32 devices in a mesh: dp: 8 (over z, y), tensor: 4 (over x, core).
Axes of the slice: x: 2, y: 2, z: 4, core: 2. Of those that a mesh axis runs over, the one named last changes fastest.
Arguments:
- block_input: bfloat16 [3072, 2560], P('dp', 'tensor'), may hold values from -6 to 6
- gate_act: bfloat16 [3072, 6912], P('dp', 'tensor'), may hold values from -8 to 8
- grad_out: bfloat16 [3072, 2560], P('dp', 'tensor'), may hold values from -8 to 8
- up_weight: bfloat16 [2560, 6912], P('dp', 'tensor'), may hold values from -0.125 to 0.125
- down_weight: bfloat16 [6912, 2560], P('tensor', 'dp'), may hold values from -0.078125 to 0.078125
- quant_step: float32 [6912], P('tensor'), as said below
- round_logit: float32 [2560, 6912], P('dp', 'tensor'), may hold values from -48 to 48
- grid_offset: bfloat16 [2560, 6912], P('dp', 'tensor'), may hold values from 0 to 1
Outputs:
- block_output: bfloat16 [3072, 2560], P('dp', 'tensor')
- fisher: bfloat16 [3072, 6912], P('dp', 'tensor')
- grad_logit: float32 [2560, 6912], P('dp', 'tensor')
- loss: float32 [], replicated
The draws below stay inside these ranges and needn't reach their ends.
Inputs may be any that keep to these rules, and one draw needn't show every extreme that they name: `quant_step`: positive steps between 0.8 and 3.2 divided by the square root of 2560.
All inputs are finite; a program needn't handle non-finite values.
Results may differ from the reference program's by a relative error of at most 0.022.
Values may be sent and summed in bfloat16 or wider, within the bound.
No kernel may reach another device: no remote copies, remote signals or barrier semaphores. Data moves between devices by JAX's collectives and lax.ppermute only.
A program may use at most 128 MiB of HBM per device.

```python
import jax
import jax.numpy as jnp
from jax import lax

D = 2560
FFW = 6912
TOK_DEV = 384
TOKENS = 3072
N_DP = 8
N_TENSOR = 4


def draw_grad_out(key, part):
    key_noise, key_rows = jax.random.split(jax.random.fold_in(key, 11), 2)
    position = jnp.arange(TOKENS, dtype=jnp.float32) / max(TOKENS - 1, 1)
    jitter = jax.random.uniform(key_rows, (TOKENS,), jnp.float32)
    noise = jnp.clip(jax.random.normal(key_noise, (TOKENS, D), jnp.float32), -4.0, 4.0)
    row_scale = 0.3 * jnp.sqrt(10.0 ** (0.5 * position + 0.5 * jitter))
    values = row_scale[:, None] * noise
    return values.astype(jnp.bfloat16)


def draw_gate_act(key, part):
    key_noise, key_cols = jax.random.split(jax.random.fold_in(key, 23), 2)
    position = jnp.arange(FFW, dtype=jnp.float32) / max(FFW - 1, 1)
    jitter = jax.random.uniform(key_cols, (FFW,), jnp.float32)
    noise = jnp.clip(jax.random.normal(key_noise, (TOKENS, FFW), jnp.float32), -4.0, 4.0)
    col_scale = 0.5 * jnp.sqrt(10.0 ** (0.5 * position + 0.5 * jitter))
    values = col_scale[None, :] * noise
    return values.astype(jnp.bfloat16)


def draw_quant_step(key, part):
    key_steps = jax.random.fold_in(key, 53)
    factor = jnp.exp(jax.random.uniform(key_steps, (FFW,), jnp.float32, jnp.log(0.8), jnp.log(3.2)))
    return factor * (1.0 / jnp.sqrt(jnp.float32(D)))


def draw_round_logit(key, part):
    key_noise, key_rows = jax.random.split(jax.random.fold_in(key, 37), 2)
    position = jnp.arange(D, dtype=jnp.float32) / max(D - 1, 1)
    jitter = jax.random.uniform(key_rows, (D,), jnp.float32, 0.8, 1.2)
    noise = jax.random.uniform(key_noise, (D, FFW), jnp.float32, -1.0, 1.0)
    amplitude = 30.0 * (0.2 / 30.0) ** position * jitter
    values = amplitude[:, None] * noise
    return values


def with_spikes(entries, own_key, source, target, parts, factor):
    owner, partner = [(jnp.arange(entries.shape[axis_at]) // (entries.shape[axis_at] // parts)).reshape([-1 if axis == axis_at else 1 for axis in range(entries.ndim)]) for axis_at in (source, target)]
    chosen = jax.random.permutation(own_key, parts)[partner]
    strong = (owner == chosen) | (owner == (partner + parts // 2) % parts)
    return jnp.where(strong, factor * entries, entries)


def shard_levels(key, extent, pieces, smallest, top_value):
    factor_of, own = 1.0, jax.random.fold_in(key, 6)
    for axis_at, shards_of in pieces:
        steps = jnp.exp(jax.random.uniform(jax.random.fold_in(own, axis_at), (shards_of,), jnp.float32, smallest / len(pieces), top_value / len(pieces)))
        factor_of = factor_of * jnp.repeat(steps, extent[axis_at] // shards_of).reshape([-1 if axis == axis_at else 1 for axis in range(len(extent))])
    return factor_of


def normal_values(stream_key, shape, spread, most, shards=(), held_as=jnp.bfloat16):
    drawn = spread * jax.random.normal(stream_key, shape, jnp.float32)
    if shards:
        drawn = drawn * shard_levels(stream_key, shape, shards, -0.22, 0.18)
    return jnp.clip(drawn, -most, most).astype(held_as)


def gaussian_with(rng, dims, deviation, reach, shards, heavy, kind=jnp.bfloat16):
    result = deviation * jax.random.normal(rng, dims, jnp.float32)
    if shards:
        result = result * shard_levels(rng, dims, shards, -0.22, 0.18)
    return jnp.clip(with_spikes(result, jax.random.fold_in(rng, 3), *heavy), -reach, reach).astype(kind)


def setup_inputs(seed: int = 0) -> dict:
    seeds = jax.random.split(jax.random.key(seed), 9)
    return {
        "block_input": gaussian_with(seeds[0], (TOKENS, D), 1.0, 6.0, ((0, 8), (1, 4)), (0, 1, 8, 2.0)),
        "gate_act": draw_gate_act(jax.random.fold_in(seeds[8], 71), 0),
        "grad_out": draw_grad_out(jax.random.fold_in(seeds[8], 71), 0),
        "up_weight": normal_values(seeds[3], (D, FFW), D ** -0.5, 0.125, ((0, 8), (1, 4))),
        "down_weight": normal_values(seeds[4], (FFW, D), FFW ** -0.5, 0.078125, ((0, 4), (1, 8))),
        "quant_step": draw_quant_step(jax.random.fold_in(seeds[8], 71), 0),
        "round_logit": draw_round_logit(jax.random.fold_in(seeds[8], 71), 0),
        "grid_offset": jnp.clip(1.0 * jax.random.uniform(seeds[7], (D, FFW), jnp.float32) ** shard_levels(seeds[7], (D, FFW), ((0, 8), (1, 4)), -0.2, 0.2), 0.0, 1.0).astype(jnp.bfloat16),
    }


reg_weight = 0.5


def rounded(values):
    low = lax.optimization_barrier(values.astype(jnp.bfloat16))
    return low.astype(jnp.float32)


def reference(block_input, gate_act, grad_out, up_weight, down_weight, quant_step, round_logit, grid_offset):
    up_proj = jnp.dot(block_input, up_weight, preferred_element_type=jnp.float32)
    hidden = (gate_act.astype(jnp.float32) * up_proj).astype(jnp.bfloat16)
    group_size = FFW // N_TENSOR
    out_total = jnp.zeros((TOKENS, D), jnp.float32)
    for group in range(N_TENSOR):
        lower = group * group_size
        partial_out = jnp.dot(hidden[:, lower:lower + group_size], down_weight[lower:lower + group_size, :], preferred_element_type=jnp.float32)
        out_total = out_total + rounded(partial_out)
    block_output = out_total.astype(jnp.bfloat16)
    grad_hidden = lax.dot_general(grad_out, down_weight, (((1,), (1,)), ((), ())), preferred_element_type=jnp.float32)
    fisher = ((grad_hidden * gate_act.astype(jnp.float32)) ** 2).astype(jnp.bfloat16)
    fisher_vals = fisher.astype(jnp.float32)
    soft_bits = jax.nn.sigmoid(round_logit)
    weight_delta = (quant_step[None, :] * (soft_bits - grid_offset.astype(jnp.float32))).astype(jnp.bfloat16)
    residual = jnp.dot(block_input, weight_delta, preferred_element_type=jnp.float32)
    weighted = (fisher_vals * residual).astype(jnp.bfloat16)
    input_groups = block_input.reshape(N_DP, TOK_DEV, D)
    weighted_groups = weighted.reshape(N_DP, TOK_DEV, FFW)

    def add_group(running, operands):
        rows_in, rows_weighted = operands
        product = lax.dot_general(rows_in, rows_weighted, (((0,), (0,)), ((), ())), preferred_element_type=jnp.float32)
        return running + rounded(product), None

    grad_sum, unused = lax.scan(add_group, jnp.zeros((D, FFW), jnp.float32), (input_groups, weighted_groups))
    total_cells = TOKENS * FFW
    weight_cells = D * FFW
    fisher_mean = jnp.sum(fisher_vals) / total_cells
    centered = 2.0 * soft_bits - 1.0
    sig_slope = soft_bits * (1.0 - soft_bits)
    grad_logit = grad_sum * (2.0 / fisher_mean) * quant_step[None, :] * sig_slope - reg_weight * 8.0 * centered ** 3 * sig_slope
    recon_total = jnp.sum(fisher_vals * residual * residual)
    reg_total = jnp.sum(1.0 - (centered * centered) ** 2)
    loss = recon_total / (fisher_mean * total_cells) + reg_weight * reg_total / weight_cells
    return block_output, fisher, grad_logit, loss
```

```python
import jax
import jax.numpy as jnp
from jax import lax
from jax.sharding import PartitionSpec as P

reg_weight = 0.5
SPLIT_BIT = 1


def swap(values, axis, bit):
    pairs = [(i, i ^ (1 << bit)) for i in range(lax.axis_size(axis))]
    return lax.ppermute(values, axis, pairs)


def bit_of(axis, bit):
    return (lax.axis_index(axis) >> bit) & 1


def ordered(flag, mine, theirs):
    return jnp.where(flag == 0, mine, theirs), jnp.where(flag == 0, theirs, mine)


def pick(flag, first, second):
    return jnp.where(flag == 0, first, second)


def n_bits(size):
    return size.bit_length() - 1


def gather_bits(values, axis, bits, have=()):
    have = list(have)
    for bit in bits:
        at = sum(1 for b in have if b > bit)
        theirs = swap(values, axis, bit)
        values = jnp.stack(ordered(bit_of(axis, bit), values, theirs), axis=at)
        have = sorted(have + [bit], reverse=True)
    return values


def gather_weight(shard):
    rows, cols = shard.shape
    half = cols // 2
    nb = n_bits(lax.axis_size("dp"))
    flag = bit_of("dp", SPLIT_BIT)
    keep = pick(flag, shard[:, :half], shard[:, half:])
    send = pick(flag, shard[:, half:], shard[:, :half])
    theirs = swap(send, "dp", SPLIT_BIT)
    pair = jnp.stack(ordered(flag, keep, theirs))
    order = [b for b in range(nb - 1, -1, -1) if b > SPLIT_BIT] + [b for b in range(SPLIT_BIT)]
    full = gather_bits(pair, "dp", order, [SPLIT_BIT])
    return full.reshape(-1, half)


def gather_tokens(shard):
    pair = jnp.concatenate(
        ordered(bit_of("dp", SPLIT_BIT), shard, swap(shard, "dp", SPLIT_BIT)), axis=0
    )
    nt = n_bits(lax.axis_size("tensor"))
    full = gather_bits(pair, "tensor", list(range(nt - 1, -1, -1)))
    full = full.reshape(-1, *pair.shape)
    return jnp.concatenate([full[i] for i in range(full.shape[0])], axis=1)


def take_bit(values, flag, at):
    lower = lax.index_in_dim(values, 0, at, keepdims=False)
    upper = lax.index_in_dim(values, 1, at, keepdims=False)
    return pick(flag, lower, upper), pick(flag, upper, lower)


def reduce_bits(values, axis, bits, have):
    have = list(have)
    for bit in bits:
        at = have.index(bit)
        keep, send = take_bit(values, bit_of(axis, bit), at)
        theirs = swap(send, axis, bit)
        values = (keep.astype(jnp.float32) + theirs.astype(jnp.float32)).astype(jnp.bfloat16)
        have.pop(at)
    return values


def body(
    block_input, gate_act, grad_out, up_weight, down_weight, quant_step, round_logit, grid_offset
):
    n_dp, n_tensor = lax.axis_size("dp"), lax.axis_size("tensor")
    nb, nt = n_bits(n_dp), n_bits(n_tensor)
    tok, cols = gate_act.shape
    half = cols // 2
    rows = up_weight.shape[0]
    depth = rows * n_dp
    feats = block_input.shape[1]
    flag = bit_of("dp", SPLIT_BIT)

    down_full = gather_weight(down_weight.T)
    out_grads = gather_tokens(grad_out)

    gate_keep = pick(flag, gate_act[:, :half], gate_act[:, half:])
    gate_send = pick(flag, gate_act[:, half:], gate_act[:, :half])
    gate = jnp.concatenate(ordered(flag, gate_keep, swap(gate_send, "dp", SPLIT_BIT)), axis=0)
    gate_vals = gate.astype(jnp.float32)

    soft_bits = jax.nn.sigmoid(round_logit)
    weight_delta = (quant_step[None, :] * (soft_bits - grid_offset.astype(jnp.float32))).astype(
        jnp.bfloat16
    )
    delta_full = gather_weight(weight_delta)
    features = gather_tokens(block_input)

    grad_hidden = jnp.dot(out_grads, down_full, preferred_element_type=jnp.float32)
    fisher = ((grad_hidden * gate_vals) ** 2).astype(jnp.bfloat16)
    fisher_vals = fisher.astype(jnp.float32)
    fisher_local = jnp.sum(fisher_vals)

    residual = jnp.dot(features, delta_full, preferred_element_type=jnp.float32)
    weighted = (fisher_vals * residual).astype(jnp.bfloat16)
    recon_local = jnp.sum(fisher_vals * residual * residual)
    centered = 2.0 * soft_bits - 1.0
    reg_local = jnp.sum(1.0 - (centered * centered) ** 2)

    grad_part = lax.dot_general(
        features, weighted, (((0,), (0,)), ((), ())), preferred_element_type=jnp.float32
    ).astype(jnp.bfloat16)
    grad_part = grad_part.reshape((2,) * nb + (rows, half))
    order = [b for b in range(SPLIT_BIT)] + [b for b in range(SPLIT_BIT + 1, nb)]
    grad_part = reduce_bits(grad_part, "dp", order, list(range(nb - 1, -1, -1)))
    keep, send = take_bit(grad_part, flag, 0)
    theirs = swap(send, "dp", SPLIT_BIT)
    grad_sum = jnp.concatenate(ordered(flag, keep, theirs), axis=1).astype(jnp.float32)

    fish_keep, fish_send = take_bit(fisher.reshape(2, tok, half), flag, 0)
    fisher_out = jnp.concatenate(
        ordered(flag, fish_keep, swap(fish_send, "dp", SPLIT_BIT)), axis=1
    )

    up_full = gather_weight(up_weight)
    up_proj = jnp.dot(features, up_full, preferred_element_type=jnp.float32)
    hidden = (gate_vals * up_proj).astype(jnp.bfloat16)
    out_part = lax.dot_general(
        hidden, down_full, (((1,), (1,)), ((), ())), preferred_element_type=jnp.float32
    ).astype(jnp.bfloat16)
    out_part = jnp.stack([out_part[:, i * feats : (i + 1) * feats] for i in range(n_tensor)])
    out_part = out_part.reshape((2,) * nt + (2 * tok, feats))
    out_part = reduce_bits(out_part, "tensor", list(range(nt)), list(range(nt - 1, -1, -1)))
    out_part = out_part.reshape(2, tok, feats)
    block_output = reduce_bits(out_part, "dp", [SPLIT_BIT], [SPLIT_BIT])

    sums = jnp.stack([fisher_local, recon_local, reg_local])
    for axis, count in (("dp", nb), ("tensor", nt)):
        for bit in range(count):
            sums = sums + swap(sums, axis, bit)
    fisher_sum, recon_total, reg_total = sums[0], sums[1], sums[2]
    total_cells = n_dp * n_tensor * tok * cols
    weight_cells = depth * n_tensor * cols
    fisher_mean = fisher_sum / total_cells
    sig_slope = soft_bits * (1.0 - soft_bits)
    grad_logit = (
        grad_sum * (2.0 / fisher_mean) * quant_step[None, :] * sig_slope
        - reg_weight * 8.0 * centered**3 * sig_slope
    )
    loss = recon_total / (fisher_mean * total_cells) + reg_weight * reg_total / weight_cells
    return (block_output, fisher_out, grad_logit, loss)


def solution(mesh):
    placed = (
        P("dp", "tensor"),
        P("dp", "tensor"),
        P("dp", "tensor"),
        P("dp", "tensor"),
        P("tensor", "dp"),
        P("tensor"),
        P("dp", "tensor"),
        P("dp", "tensor"),
    )
    return jax.shard_map(
        body,
        mesh=mesh,
        in_specs=placed,
        out_specs=(P("dp", "tensor"), P("dp", "tensor"), P("dp", "tensor"), P()),
        check_vma=False,
    )
```

```python
import jax
import jax.numpy as jnp
from jax import lax
from jax.sharding import PartitionSpec as P

reg_weight = 0.5


def swap(values, axis, bit):
    pairs = [(i, i ^ (1 << bit)) for i in range(lax.axis_size(axis))]
    return lax.ppermute(values, axis, pairs)


def bit_of(axis, bit):
    return (lax.axis_index(axis) >> bit) & 1


def n_bits(size):
    return size.bit_length() - 1


def pick(flag, first, second):
    return jnp.where(flag == 0, first, second)


def ordered(flag, mine, theirs):
    return pick(flag, mine, theirs), pick(flag, theirs, mine)


def halves(values):
    half = values.shape[1] // 2
    return values[:, :half], values[:, half:]


def side(values, flag):
    return pick(flag, *halves(values))


def wide(left, right):
    return jnp.concatenate([left, right], axis=1)


def spread_columns(shard):
    y, z = bit_of("dp", 0), bit_of("dp", 1)
    theirs = swap(side(shard, 1 - y), "dp", 0)
    own = side(shard, y)
    near = wide(side(own, z), side(theirs, z))
    far = swap(wide(side(own, 1 - z), side(theirs, 1 - z)), "dp", 1)
    return near, far


def collect_columns(near, away):
    y, z = bit_of("dp", 0), bit_of("dp", 1)
    back = swap(away, "dp", 1)
    near_own, near_other = halves(near)
    back_own, back_other = halves(back)
    theirs = swap(wide(*ordered(z, near_other, back_other)), "dp", 0)
    return wide(*ordered(y, wide(*ordered(z, near_own, back_own)), theirs))


def block_shift(nb, nt):
    return (lax.axis_index("dp") >> 1) ^ (lax.axis_index("tensor") << (nb - 1 - nt))


def gather_weight(shard, nb, nt):
    pieces = list(spread_columns(shard))
    for bit in range(2, nb):
        pieces = pieces + [swap(piece, "dp", bit) for piece in pieces]
    y = bit_of("dp", 0)
    rows, cols = pieces[0].shape
    shift = block_shift(nb, nt)
    full = jnp.zeros((2 * rows * len(pieces), cols // 2), shard.dtype)
    for index, piece in enumerate(pieces):
        block = jnp.concatenate(ordered(y, *halves(piece)), axis=0)
        full = lax.dynamic_update_slice(full, block, ((index ^ shift) * 2 * rows, 0))
    return full


def scatter_weight(full, nb, nt):
    y = bit_of("dp", 0)
    count = 1 << (nb - 1)
    rows = full.shape[0] // (2 * count)
    shift = block_shift(nb, nt)

    def piece(index):
        block = lax.dynamic_slice(
            full, ((index ^ shift) * 2 * rows, 0), (2 * rows, full.shape[1])
        )
        return wide(*ordered(y, block[:rows], block[rows:]))

    pieces = [piece(index) for index in range(count)]
    for bit in range(nb - 1, 1, -1):
        keep = len(pieces) // 2
        pieces = [
            (mine.astype(jnp.float32) + swap(theirs, "dp", bit).astype(jnp.float32)).astype(
                jnp.bfloat16
            )
            for mine, theirs in zip(pieces[:keep], pieces[keep:])
        ]
    return collect_columns(*pieces)


def gather_features(chunk, nt):
    blocks = [chunk]
    for bit in range(nt - 1, -1, -1):
        got = [swap(block, "tensor", bit) for block in blocks]
        blocks = [b for two in zip(blocks, got) for b in two]
    return jnp.concatenate(blocks, axis=1)


def gather_tokens(shard, nt):
    chunks = []
    for chunk in (shard, swap(shard, "dp", 1)):
        chunk = jnp.concatenate([chunk, swap(chunk, "dp", 0)], axis=0)
        chunks.append(gather_features(chunk, nt))
    return jnp.concatenate(chunks, axis=0)


def add_rounded(mine, theirs):
    return (mine.astype(jnp.float32) + theirs.astype(jnp.float32)).astype(jnp.bfloat16)


def scatter_output(part, nt):
    count = 1 << nt
    tok, feats = part.shape[0] // 4, part.shape[1] // count
    chunks = []
    for at in (0, 1):
        rows = part[2 * tok * at : 2 * tok * (at + 1)]
        blocks = [rows[:, i * feats : (i + 1) * feats] for i in range(count)]
        for bit in range(nt):
            blocks = [
                add_rounded(mine, swap(theirs, "tensor", bit))
                for mine, theirs in zip(blocks[::2], blocks[1::2])
            ]
        rows = blocks[0]
        chunks.append(add_rounded(rows[:tok], swap(rows[tok:], "dp", 0)))
    return add_rounded(chunks[0], swap(chunks[1], "dp", 1))


def body(
    block_input, gate_act, grad_out, up_weight, down_weight, quant_step, round_logit, grid_offset
):
    n_dp, n_tensor = lax.axis_size("dp"), lax.axis_size("tensor")
    nb, nt = n_bits(n_dp), n_bits(n_tensor)
    tok, cols = gate_act.shape
    depth = up_weight.shape[0] * n_dp

    down_full = gather_weight(down_weight.T, nb, nt)
    out_grads = gather_tokens(grad_out, nt)
    gate = jnp.concatenate(
        [part for pair in spread_columns(gate_act) for part in halves(pair)], axis=0
    )
    gate_vals = gate.astype(jnp.float32)

    soft_bits = jax.nn.sigmoid(round_logit)
    weight_delta = (quant_step[None, :] * (soft_bits - grid_offset.astype(jnp.float32))).astype(
        jnp.bfloat16
    )
    delta_full = gather_weight(weight_delta, nb, nt)
    features = gather_tokens(block_input, nt)

    grad_hidden = jnp.dot(out_grads, down_full, preferred_element_type=jnp.float32)
    fisher = ((grad_hidden * gate_vals) ** 2).astype(jnp.bfloat16)
    fisher_vals = fisher.astype(jnp.float32)
    fisher_local = jnp.sum(fisher_vals)

    residual = jnp.dot(features, delta_full, preferred_element_type=jnp.float32)
    weighted = (fisher_vals * residual).astype(jnp.bfloat16)
    recon_local = jnp.sum(fisher_vals * residual * residual)
    centered = 2.0 * soft_bits - 1.0
    reg_local = jnp.sum(1.0 - (centered * centered) ** 2)

    grad_part = lax.dot_general(
        features, weighted, (((0,), (0,)), ((), ())), preferred_element_type=jnp.float32
    ).astype(jnp.bfloat16)
    grad_sum = scatter_weight(grad_part, nb, nt).astype(jnp.float32)

    fisher_out = collect_columns(
        wide(fisher[:tok], fisher[tok : 2 * tok]), wide(fisher[2 * tok : 3 * tok], fisher[3 * tok :])
    )

    up_full = gather_weight(up_weight, nb, nt)
    up_proj = jnp.dot(features, up_full, preferred_element_type=jnp.float32)
    hidden = (gate_vals * up_proj).astype(jnp.bfloat16)
    out_part = lax.dot_general(
        hidden, down_full, (((1,), (1,)), ((), ())), preferred_element_type=jnp.float32
    ).astype(jnp.bfloat16)
    block_output = scatter_output(out_part, nt)

    sums = jnp.stack([fisher_local, recon_local, reg_local])
    for axis, count in (("dp", nb), ("tensor", nt)):
        for bit in range(count):
            sums = sums + swap(sums, axis, bit)
    fisher_sum, recon_total, reg_total = sums[0], sums[1], sums[2]
    total_cells = n_dp * n_tensor * tok * cols
    weight_cells = depth * n_tensor * cols
    fisher_mean = fisher_sum / total_cells
    sig_slope = soft_bits * (1.0 - soft_bits)
    grad_logit = (
        grad_sum * (2.0 / fisher_mean) * quant_step[None, :] * sig_slope
        - reg_weight * 8.0 * centered**3 * sig_slope
    )
    loss = recon_total / (fisher_mean * total_cells) + reg_weight * reg_total / weight_cells
    return (block_output, fisher_out, grad_logit, loss)


def solution(mesh):
    placed = (
        P("dp", "tensor"),
        P("dp", "tensor"),
        P("dp", "tensor"),
        P("dp", "tensor"),
        P("tensor", "dp"),
        P("tensor"),
        P("dp", "tensor"),
        P("dp", "tensor"),
    )
    return jax.shard_map(
        body,
        mesh=mesh,
        in_specs=placed,
        out_specs=(P("dp", "tensor"), P("dp", "tensor"), P("dp", "tensor"), P()),
        check_vma=False,
    )
```

```python
import functools

import jax
import jax.numpy as jnp
from jax import lax
from jax.experimental import pallas as pl
from jax.experimental.pallas import tpu as pltpu
from jax.sharding import PartitionSpec as P

reg_weight = 0.5

ORDER = (
    0,
    48,
    12,
    10,
    1,
    30,
    2,
    3,
    6,
    4,
    46,
    11,
    21,
    36,
    5,
    8,
    49,
    37,
    22,
    23,
    24,
    7,
    50,
    66,
    38,
    39,
    53,
    51,
    13,
    67,
    40,
    42,
    9,
    47,
    57,
    25,
    14,
    15,
    68,
    31,
    69,
    17,
    28,
    43,
    72,
    41,
    26,
    58,
    44,
    52,
    70,
    29,
    59,
    32,
    33,
    18,
    16,
    60,
    19,
    71,
    34,
    45,
    74,
    20,
    61,
    76,
    55,
    27,
    64,
    35,
    75,
    62,
    77,
    65,
    56,
    54,
    90,
    63,
    78,
    117,
    79,
    82,
    118,
    73,
    95,
    119,
    120,
    96,
    107,
    121,
    91,
    92,
    122,
    80,
    108,
    97,
    81,
    85,
    98,
    123,
    99,
    93,
    109,
    124,
    125,
    110,
    83,
    111,
    100,
    94,
    101,
    86,
    126,
    102,
    127,
    128,
    84,
    87,
    88,
    129,
    103,
    104,
    112,
    105,
    113,
    114,
    130,
    89,
    131,
    115,
    116,
    106,
)

VMEM = pl.BlockSpec(memory_space=pltpu.VMEM)
SMEM = pl.BlockSpec(memory_space=pltpu.SMEM)
PARAMS = pltpu.CompilerParams(vmem_limit_bytes=32 * 1024 * 1024)
SMALL = pltpu.CompilerParams(vmem_limit_bytes=16 * 1024 * 1024)


def swap(values, axis, bit):
    pairs = [(i, i ^ (1 << bit)) for i in range(lax.axis_size(axis))]
    return lax.ppermute(values, axis, pairs)


def bit_of(axis, bit):
    return (lax.axis_index(axis) >> bit) & 1


def n_bits(size):
    return size.bit_length() - 1


def pick(flag, first, second):
    return jnp.where(flag == 0, first, second)


def f32_dot(left, right, dims):
    return lax.dot_general(left, right, (dims, ((), ())), preferred_element_type=jnp.float32)


def add_rounded(mine, theirs, parts=1, axis=0):
    shape = list(mine.shape)
    shape[axis] //= parts
    return pl.pallas_call(
        functools.partial(add_kernel, axis),
        out_shape=[bf16(*shape)] * parts,
        in_specs=[VMEM, VMEM],
        out_specs=[VMEM] * parts,
        compiler_params=SMALL,
        name="add",
    )(mine, theirs)


def join(first, second):
    return pl.pallas_call(
        join_kernel,
        out_shape=bf16(2 * first.shape[0], first.shape[1]),
        in_specs=[VMEM, VMEM],
        out_specs=VMEM,
        compiler_params=SMALL,
        name="join",
    )(first, second)


def scalars(*values):
    return jnp.stack([jnp.asarray(value, jnp.int32) for value in values])


def bf16(*shape):
    return jax.ShapeDtypeStruct(shape, jnp.bfloat16)


def store_halves(flag, values, send, keep, axis):
    half = values.shape[axis] // 2
    lower, upper = (values[:half], values[half:]) if axis == 0 else (values[:, :half], values[:, half:])

    @pl.when(flag == 0)
    def _():
        keep[...] = lower
        send[...] = upper

    @pl.when(flag != 0)
    def _():
        keep[...] = upper
        send[...] = lower


def split_kernel(flags, shard, send, keep):
    store_halves(flags[0], shard[...], send, keep, 1)


def delta_kernel(flags, logit, offset, step, send, keep):
    soft_bits = jax.nn.sigmoid(logit[...])
    delta = step[...] * (soft_bits - offset[...].astype(jnp.float32))
    store_halves(flags[0], delta.astype(jnp.bfloat16), send, keep, 1)


def half_kernel(flags, shard, send, keep):
    store_halves(flags[0], shard[...], send, keep, 0)


def pair_kernel(turn, flags, own, theirs, near, far):
    own, theirs = (own[...].T, theirs[...].T) if turn else (own[...], theirs[...])
    half, cols = own.shape[0] // 2, own.shape[1]
    for flag in (0, 1):

        @pl.when(flags[0] == flag)
        def _(flag=flag):
            for lower, out in ((0, near), (half, far)):
                start = half - lower if flag else lower
                for order, (left, right) in enumerate(((own, theirs), (theirs, own))):

                    @pl.when(flags[1] == order)
                    def _(start=start, out=out, left=left, right=right):
                        out[:, :cols] = left[start : start + half]
                        out[:, cols:] = right[start : start + half]


def join_kernel(first, second, out):
    rows = first.shape[0]
    out[:rows, :] = first[...]
    out[rows:, :] = second[...]


def add_kernel(axis, mine, theirs, *outs):
    total = mine[...].astype(jnp.float32) + theirs[...].astype(jnp.float32)
    total = total.astype(jnp.bfloat16)
    size = total.shape[axis] // len(outs)
    for i, out in enumerate(outs):
        at = slice(i * size, (i + 1) * size)
        out[...] = total[at] if axis == 0 else total[:, at]


def rows_kernel(flags, near, back, own, other):
    half, cols = near.shape[0], near.shape[1] // 2
    for z, (first, second) in enumerate(((near, back), (back, near))):

        @pl.when(flags[1] == z)
        def _(first=first, second=second):
            left = jnp.concatenate([first[:, :cols], second[:, :cols]], axis=0).T
            right = jnp.concatenate([first[:, cols:], second[:, cols:]], axis=0).T

            @pl.when(flags[0] == 0)
            def _():
                own[...] = left
                other[...] = right

            @pl.when(flags[0] != 0)
            def _():
                own[...] = right
                other[...] = left


def place(flags, pieces, whole):
    for index, piece in enumerate(pieces):
        whole[index ^ flags[0]] = piece[...]


def times_weight(whole, blocks):
    count, _, wide = whole.shape
    per = count // len(blocks)
    total = None
    for i in range(count):
        block = blocks[i // per]
        at = (i % per) * wide
        part = f32_dot(whole[i], block[:, at : at + wide], ((1,), (1,)))
        total = part if total is None else total + part
    return total


def fisher_kernel(count, *refs):
    flags, pieces, refs = refs[0], refs[1 : count + 1], refs[count + 1 :]
    blocks, (gate, fisher, total, whole) = refs[:-4], refs[-4:]
    place(flags, pieces, whole)
    grads = times_weight(whole, blocks)
    value = ((grads * gate[...].astype(jnp.float32)) ** 2).astype(jnp.bfloat16)
    fisher[...] = value
    total[0, 0] = jnp.sum(value.astype(jnp.float32))


def grad_kernel(count, *refs):
    flags, pieces, refs = refs[0], refs[1 : count + 1], refs[count + 1 :]
    half = (len(refs) - count - 4) // 2
    blocks, (fisher_a, fisher_b), refs = refs[: 2 * half], refs[2 * half : 2 * half + 2], refs[2 * half + 2 :]
    grads, (total, whole) = refs[:count], refs[count:]
    place(flags, pieces, whole)
    weighted, sums = [], []
    for chunk, fisher in ((blocks[:half], fisher_a), (blocks[half:], fisher_b)):
        residual = times_weight(whole, chunk)
        value = fisher[...].astype(jnp.float32) * residual
        weighted.append(value.astype(jnp.bfloat16))
        sums.append(jnp.sum(value * residual))
    total[0, 0] = sums[0] + sums[1]
    wide = whole.shape[2]
    per = count // half
    for i in range(count):
        at = (i % per) * wide
        part = f32_dot(weighted[0], blocks[i // per][:, at : at + wide], ((1,), (0,)))
        part += f32_dot(weighted[1], blocks[half + i // per][:, at : at + wide], ((1,), (0,)))
        part = part.astype(jnp.bfloat16)
        for j in range(count):

            @pl.when(flags[0] == i ^ j)
            def _(part=part, j=j):
                grads[j][...] = part


def output_kernel(count, *refs):
    flags, ups, downs = refs[0], refs[1 : count + 1], refs[count + 1 : 2 * count + 1]
    refs = refs[2 * count + 1 :]
    blocks, (gate, keep, send, whole) = refs[:-4], refs[-4:]
    place(flags, ups, whole)
    hidden = times_weight(whole, blocks) * gate[...].astype(jnp.float32)
    hidden = hidden.astype(jnp.bfloat16)
    place(flags, downs, whole)
    feats, wide = blocks[0].shape[1], whole.shape[2]
    per = count // len(blocks)
    for i in range(count):
        k = i // per
        at = (k >> 1) * feats + (i % per) * wide
        out = send if k & 1 else keep
        part = f32_dot(hidden, whole[i], ((0,), (0,)))
        out[:, at : at + wide] = part.astype(jnp.bfloat16)


class Plan:
    def __init__(self):
        self.steps, self.got, self.flying, self.token = {}, {}, {}, None

    def tie(self, values):
        values, self.token = lax.optimization_barrier((values, self.token))
        return values

    def exchange(self, name, axis, bit, source):
        def start():
            self.flying[name] = swap(self.tie(source()), axis, bit)

        def wait():
            self.got[name] = self.tie(self.flying.pop(name))

        self.steps["s " + name], self.steps["w " + name] = start, wait

    def compute(self, name, function, tied=True):
        def run():
            values = function()
            self.got[name] = self.tie(values) if tied else values

        self.steps["c " + name] = run

    def run(self, token, order):
        self.token = token
        steps = list(self.steps.values())
        if len(order) != len(steps):
            order = range(len(steps))
        for number in order:
            steps[number]()
        return self.got


def plan_pair(plan, name, first, order, turn):
    got = plan.got
    plan.compute("p" + name, first)
    plan.exchange(name + "_y", "dp", 0, lambda: got["p" + name][0])

    def pair():
        own, theirs = got["p" + name][1], got[name + "_y"]
        rows, cols = own.shape[::-1] if turn else own.shape
        out = bf16(rows // 2, 2 * cols)
        return pl.pallas_call(
            functools.partial(pair_kernel, turn),
            out_shape=(out, out),
            in_specs=[SMEM, VMEM, VMEM],
            out_specs=(VMEM, VMEM),
            compiler_params=SMALL,
            name="pair",
        )(scalars(bit_of("dp", 1), order), own, theirs)

    plan.compute("k" + name, pair)
    plan.exchange(name + "_zl", "dp", 1, lambda: got["k" + name][1])


def plan_weight(plan, name, first, nb):
    got = plan.got
    plan_pair(plan, name, first, bit_of("dp", 0), True)
    pieces = [lambda: got["k" + name][0], lambda: got[name + "_zl"]]
    for bit in range(2, nb):
        for piece in list(pieces):
            key = name + "_h" + str(len(pieces) - 2)
            plan.exchange(key, "dp", bit, piece)
            pieces.append(lambda key=key: got[key])
    return lambda: [piece() for piece in pieces]


def plan_tokens(plan, name, shard, nt):
    got, chunks = plan.got, {}
    plan.exchange(name + "b_zl", "dp", 1, lambda: shard)
    for chunk, own in (("a", lambda: shard), ("b", lambda: got[name + "b_zl"])):
        key = name + chunk
        plan.exchange(key + "_y", "dp", 0, own)
        plan.compute(
            "c" + key,
            lambda own=own, key=key: join(own(), got[key + "_y"]),
        )
        blocks = ["c" + key]
        for bit in range(nt - 1, -1, -1):
            new = []
            for index, block in enumerate(blocks):
                part = key + "_t" + str(bit) + str(index)
                plan.exchange(part, "tensor", bit, lambda block=block: got[block])
                new += [block, part]
            blocks = new
        chunks[chunk] = blocks
    return lambda chunk: [got[key] for key in chunks[chunk]]


def plan_collect(plan, name, near, away):
    got = plan.got
    y, z = bit_of("dp", 0), bit_of("dp", 1)
    plan.exchange(name + "_zl", "dp", 1, away)

    def rest(at):
        cols = near().shape[1] // 2
        own, back = (part[:, at * cols : (at + 1) * cols] for part in (near(), got[name + "_zl"]))
        return jnp.concatenate([pick(z, own, back), pick(z, back, own)], axis=0)

    plan.compute("p" + name, lambda: rest(1))
    plan.exchange(name + "_y", "dp", 0, lambda: got["p" + name])

    def whole():
        own, theirs = rest(0), got[name + "_y"]
        return jnp.concatenate([pick(y, own, theirs), pick(y, theirs, own)], axis=0)

    return whole


def plan_scatter(plan, full, nb):
    got = plan.got
    y, z = bit_of("dp", 0), bit_of("dp", 1)
    half, number, pieces = 1 << (nb - 2), 0, []
    for index in range(2 * half):
        pieces.append(lambda index=index: full()[index])
    for bit in range(nb - 1, 1, -1):
        half = len(pieces) // 2
        sums = []
        for index in reversed(range(half)):
            name = "R_h" + str(number)
            plan.exchange(name, "dp", bit, pieces[half + index])
            plan.compute(
                "a" + str(number),
                lambda mine=pieces[index], name=name: add_rounded(mine(), got[name])[0],
            )
            sums.insert(0, lambda key="a" + str(number): got[key])
            number += 1
        pieces = sums
    near, away = pieces
    plan.exchange("R_zl", "dp", 1, away)

    def rows():
        out = bf16(near().shape[1] // 2, 2 * near().shape[0])
        return pl.pallas_call(
            rows_kernel,
            out_shape=(out, out),
            in_specs=[SMEM, VMEM, VMEM],
            out_specs=(VMEM, VMEM),
            compiler_params=SMALL,
            name="rows",
        )(scalars(y, z), near(), got["R_zl"])

    plan.compute("ry", rows)
    plan.exchange("R_y", "dp", 0, lambda: got["ry"][1])

    def whole():
        own, theirs = got["ry"][0], got["R_y"]
        return jnp.concatenate([pick(y, own, theirs), pick(y, theirs, own)], axis=1)

    return whole


def plan_output(plan, part, tok, nt):
    got = plan.got
    for chunk in "ba":
        key = "O" + chunk
        plan.compute("kC" + chunk, lambda chunk=chunk: part(chunk))
        plan.exchange(key + "_t0", "tensor", 0, lambda chunk=chunk: got["kC" + chunk][1])
        last = "o0" + chunk
        plan.compute(
            last,
            lambda chunk=chunk, key=key: add_rounded(
                got["kC" + chunk][0], got[key + "_t0"], 2, int(nt > 1)
            ),
        )
        for bit in range(nt - 1, 0, -1):
            name, step = key + "_t" + str(bit), "o" + str(bit) + chunk
            plan.exchange(name, "tensor", bit, lambda last=last: got[last][1])
            plan.compute(
                step,
                lambda last=last, name=name, bit=bit: add_rounded(
                    got[last][0], got[name], 2, int(bit > 1)
                ),
            )
            last = step
        plan.exchange(key + "_y", "dp", 0, lambda last=last: got[last][1])
        plan.compute(
            "oy" + chunk,
            lambda last=last, key=key: add_rounded(got[last][0], got[key + "_y"])[0],
        )
        if chunk == "b":
            plan.exchange("O_zl", "dp", 1, lambda: got["oyb"])
    return lambda: add_rounded(got["oya"], got["O_zl"])[0]


def body(
    block_input, gate_act, grad_out, up_weight, down_weight, quant_step, round_logit, grid_offset
):
    n_dp, n_tensor = lax.axis_size("dp"), lax.axis_size("tensor")
    nb, nt = n_bits(n_dp), n_bits(n_tensor)
    tok, cols = gate_act.shape
    half, quarter = cols // 2, cols // 4
    rows = up_weight.shape[0]
    depth = rows * n_dp
    count = n_dp // 2
    y = bit_of("dp", 0)
    shift = (lax.axis_index("dp") >> 1) ^ (lax.axis_index("tensor") << (nb - 1 - nt))

    soft_bits = jax.nn.sigmoid(round_logit)
    centered = 2.0 * soft_bits - 1.0
    reg_local = jnp.sum(1.0 - (centered * centered) ** 2)

    def split(name, kernel, out, *operands):
        return pl.pallas_call(
            kernel,
            out_shape=(out, out),
            in_specs=[SMEM] + [VMEM] * len(operands),
            out_specs=(VMEM, VMEM),
            compiler_params=SMALL,
            name=name,
        )(scalars(y), *operands)

    plan = Plan()
    got = plan.got
    out = bf16(rows, half)
    down = plan_weight(plan, "D", lambda: split("split", split_kernel, out, down_weight.T), nb)
    grads = plan_tokens(plan, "G", grad_out, nt)
    plan_pair(
        plan, "g", lambda: split("split", half_kernel, bf16(half, tok), gate_act.T), 0, False
    )
    gate = lambda chunk: got["kg"][0] if chunk == "a" else got["g_zl"]
    delta = plan_weight(
        plan,
        "T",
        lambda: split(
            "delta", delta_kernel, out, round_logit, grid_offset, quant_step[None, :]
        ),
        nb,
    )
    features = plan_tokens(plan, "X", block_input, nt)
    up = plan_weight(plan, "U", lambda: split("split", split_kernel, out, up_weight), nb)
    whole = pltpu.VMEM((count, quarter, 2 * rows), jnp.bfloat16)

    def matmuls(name, kernel, out_shape, out_specs, *operands):
        return pl.pallas_call(
            functools.partial(kernel, count),
            out_shape=out_shape,
            in_specs=[SMEM] + [VMEM] * len(operands),
            out_specs=out_specs,
            scratch_shapes=[whole],
            compiler_params=PARAMS,
            name=name,
        )(scalars(shift), *operands)

    one = jax.ShapeDtypeStruct((1, 1), jnp.float32)
    for chunk in "ab":
        plan.compute(
            "kA" + chunk,
            lambda chunk=chunk: matmuls(
                "fisher_matmul",
                fisher_kernel,
                (bf16(quarter, 2 * tok), one),
                (VMEM, SMEM),
                *down(),
                *grads(chunk),
                gate(chunk),
            ),
        )
    fisher = lambda chunk: got["kA" + chunk][0]
    plan.compute(
        "kB",
        lambda: matmuls(
            "grad_matmul",
            grad_kernel,
            [bf16(quarter, 2 * rows)] * count + [one],
            [VMEM] * count + [SMEM],
            *delta(),
            *features("a"),
            *features("b"),
            fisher("a"),
            fisher("b"),
        ),
    )
    grad_rows = plan_scatter(plan, lambda: got["kB"][:-1], nb)
    fisher_rows = plan_collect(plan, "f", lambda: fisher("a"), lambda: fisher("b"))
    pair = bf16(2 * tok, depth // 2)
    out_rows = plan_output(
        plan,
        lambda chunk: matmuls(
            "output_matmul",
            output_kernel,
            (pair, pair),
            (VMEM, VMEM),
            *up(),
            *down(),
            *features(chunk),
            gate(chunk),
        ),
        tok,
        nt,
    )

    last = lambda: jnp.concatenate(
        [got["kAa"][1] + got["kAb"][1], got["kB"][-1], reg_local[None, None]], axis=1
    )
    for axis, bits in (("dp", nb), ("tensor", nt)):
        for bit in range(bits):
            name = "s_" + axis + str(bit)
            plan.exchange(name, axis, bit, last)
            plan.compute("q" + name, lambda last=last, name=name: last() + got[name], tied=False)
            last = lambda name=name: got["q" + name]

    plan.run(lax.axis_index("dp"), ORDER)

    sums = last()[0]
    fisher_sum, recon_total, reg_total = sums[0], sums[1], sums[2]
    total_cells = n_dp * n_tensor * tok * cols
    weight_cells = depth * n_tensor * cols
    fisher_mean = fisher_sum / total_cells
    sig_slope = soft_bits * (1.0 - soft_bits)
    grad_logit = (
        grad_rows().astype(jnp.float32)
        * (2.0 / fisher_mean)
        * quant_step[None, :]
        * sig_slope
        - reg_weight * 8.0 * centered**3 * sig_slope
    )
    loss = recon_total / (fisher_mean * total_cells) + reg_weight * reg_total / weight_cells
    loss = jnp.where(plan.token < 0, -loss, loss)
    return (out_rows(), fisher_rows().T, grad_logit, loss)


def solution(mesh):
    placed = (
        P("dp", "tensor"),
        P("dp", "tensor"),
        P("dp", "tensor"),
        P("dp", "tensor"),
        P("tensor", "dp"),
        P("tensor"),
        P("dp", "tensor"),
        P("dp", "tensor"),
    )
    return jax.shard_map(
        body,
        mesh=mesh,
        in_specs=placed,
        out_specs=(P("dp", "tensor"), P("dp", "tensor"), P("dp", "tensor"), P()),
        check_vma=False,
    )
```

```python
import functools

import jax
import jax.numpy as jnp
from jax import lax
from jax.experimental import pallas as pl
from jax.experimental.pallas import tpu as pltpu
from jax.sharding import PartitionSpec as P

reg_weight = 0.5

ORDER = (
    0,
    12,
    46,
    10,
    1,
    36,
    30,
    66,
    67,
    37,
    47,
    11,
    2,
    21,
    3,
    4,
    48,
    6,
    57,
    68,
    38,
    39,
    69,
    22,
    40,
    23,
    70,
    24,
    7,
    5,
    8,
    31,
    58,
    59,
    72,
    49,
    60,
    9,
    25,
    26,
    41,
    50,
    32,
    42,
    13,
    44,
    14,
    15,
    53,
    73,
    28,
    33,
    71,
    34,
    61,
    17,
    45,
    16,
    54,
    64,
    29,
    51,
    19,
    62,
    74,
    35,
    27,
    77,
    20,
    18,
    65,
    76,
    52,
    43,
    55,
    63,
    79,
    94,
    56,
    78,
    80,
    82,
    121,
    83,
    75,
    99,
    122,
    100,
    81,
    95,
    123,
    124,
    111,
    86,
    84,
    112,
    101,
    102,
    103,
    85,
    96,
    113,
    125,
    89,
    97,
    114,
    126,
    87,
    115,
    98,
    104,
    105,
    127,
    90,
    106,
    88,
    128,
    129,
    91,
    92,
    130,
    107,
    108,
    116,
    117,
    118,
    109,
    131,
    132,
    133,
    134,
    93,
    110,
    135,
    119,
    120,
)

VMEM = pl.BlockSpec(memory_space=pltpu.VMEM)
SMEM = pl.BlockSpec(memory_space=pltpu.SMEM)
PARAMS = pltpu.CompilerParams(vmem_limit_bytes=22 * 1024 * 1024)
SMALL = pltpu.CompilerParams(vmem_limit_bytes=8 * 1024 * 1024)


def swap(values, axis, bit):
    pairs = [(i, i ^ (1 << bit)) for i in range(lax.axis_size(axis))]
    return lax.ppermute(values, axis, pairs)


def bit_of(axis, bit):
    return (lax.axis_index(axis) >> bit) & 1


def n_bits(size):
    return size.bit_length() - 1


def pick(flag, first, second):
    return jnp.where(flag == 0, first, second)


def f32_dot(left, right, dims):
    return lax.dot_general(left, right, (dims, ((), ())), preferred_element_type=jnp.float32)


def add_rounded(mine, theirs, parts=1, axis=0):
    shape = list(mine.shape)
    shape[axis] //= parts
    return pl.pallas_call(
        functools.partial(add_kernel, axis),
        out_shape=[bf16(*shape)] * parts,
        in_specs=[VMEM, VMEM],
        out_specs=[VMEM] * parts,
        compiler_params=SMALL,
        name="add",
    )(mine, theirs)


def join(first, second):
    return pl.pallas_call(
        join_kernel,
        out_shape=bf16(2 * first.shape[0], first.shape[1]),
        in_specs=[VMEM, VMEM],
        out_specs=VMEM,
        compiler_params=SMALL,
        name="join",
    )(first, second)


def scalars(*values):
    return jnp.stack([jnp.asarray(value, jnp.int32) for value in values])


def bf16(*shape):
    return jax.ShapeDtypeStruct(shape, jnp.bfloat16)


def store_halves(flag, values, send, keep, axis):
    half = values.shape[axis] // 2
    lower, upper = (values[:half], values[half:]) if axis == 0 else (values[:, :half], values[:, half:])

    @pl.when(flag == 0)
    def _():
        keep[...] = lower
        send[...] = upper

    @pl.when(flag != 0)
    def _():
        keep[...] = upper
        send[...] = lower


def split_kernel(flags, shard, send, keep):
    store_halves(flags[0], shard[...], send, keep, 1)


def delta_kernel(flags, logit, offset, step, send, keep):
    soft_bits = jax.nn.sigmoid(logit[...])
    delta = step[...] * (soft_bits - offset[...].astype(jnp.float32))
    store_halves(flags[0], delta.astype(jnp.bfloat16), send, keep, 1)


def half_kernel(flags, shard, send, keep):
    store_halves(flags[0], shard[...], send, keep, 0)


def pair_kernel(turn, flags, own, theirs, near, far):
    own, theirs = (own[...].T, theirs[...].T) if turn else (own[...], theirs[...])
    half, cols = own.shape[0] // 2, own.shape[1]
    for flag in (0, 1):

        @pl.when(flags[0] == flag)
        def _(flag=flag):
            for lower, out in ((0, near), (half, far)):
                start = half - lower if flag else lower
                for order, (left, right) in enumerate(((own, theirs), (theirs, own))):

                    @pl.when(flags[1] == order)
                    def _(start=start, out=out, left=left, right=right):
                        out[:, :cols] = left[start : start + half]
                        out[:, cols:] = right[start : start + half]


def join_kernel(first, second, out):
    rows = first.shape[0]
    out[:rows, :] = first[...]
    out[rows:, :] = second[...]


def add_kernel(axis, mine, theirs, *outs):
    total = mine[...].astype(jnp.float32) + theirs[...].astype(jnp.float32)
    total = total.astype(jnp.bfloat16)
    size = total.shape[axis] // len(outs)
    for i, out in enumerate(outs):
        at = slice(i * size, (i + 1) * size)
        out[...] = total[at] if axis == 0 else total[:, at]


def rows_kernel(flags, near, back, own, other):
    half, cols = near.shape[0], near.shape[1] // 2
    for z, (first, second) in enumerate(((near, back), (back, near))):

        @pl.when(flags[1] == z)
        def _(first=first, second=second):
            left = jnp.concatenate([first[:, :cols], second[:, :cols]], axis=0).T
            right = jnp.concatenate([first[:, cols:], second[:, cols:]], axis=0).T

            @pl.when(flags[0] == 0)
            def _():
                own[...] = left
                other[...] = right

            @pl.when(flags[0] != 0)
            def _():
                own[...] = right
                other[...] = left


def place(flags, pieces, whole):
    for index, piece in enumerate(pieces):
        whole[index ^ flags[0]] = piece[...]


def times_weight(whole, blocks):
    count, _, wide = whole.shape
    per = count // len(blocks)
    total = None
    for i in range(count):
        block = blocks[i // per]
        at = (i % per) * wide
        part = f32_dot(whole[i], block[:, at : at + wide], ((1,), (1,)))
        total = part if total is None else total + part
    return total


def fisher_kernel(count, *refs):
    flags, pieces, refs = refs[0], refs[1 : count + 1], refs[count + 1 :]
    blocks, (gate, fisher, total, whole) = refs[:-4], refs[-4:]
    place(flags, pieces, whole)
    grads = times_weight(whole, blocks)
    value = ((grads * gate[...].astype(jnp.float32)) ** 2).astype(jnp.bfloat16)
    fisher[...] = value
    total[0, 0] = jnp.sum(value.astype(jnp.float32))


def residual_kernel(count, *refs):
    flags, pieces, refs = refs[0], refs[1 : count + 1], refs[count + 1 :]
    blocks, (fisher, weighted, total, whole) = refs[:-4], refs[-4:]
    place(flags, pieces, whole)
    residual = times_weight(whole, blocks)
    value = fisher[...].astype(jnp.float32) * residual
    weighted[...] = value.astype(jnp.bfloat16)
    total[0, 0] = jnp.sum(value * residual)


def grad_kernel(count, wanted, flags, *refs):
    grads, refs = refs[-len(wanted) :], refs[: -len(wanted)]
    half = len(refs) // 2 - 1
    blocks, weighted = refs[: 2 * half], refs[2 * half :]
    wide = grads[0].shape[1]
    per = count // half
    for j, grad in zip(wanted, grads):
        for i in range(count):

            @pl.when(flags[0] == i ^ j)
            def _(i=i, grad=grad):
                at = (i % per) * wide
                first, second = blocks[i // per], blocks[half + i // per]
                part = f32_dot(weighted[0][...], first[:, at : at + wide], ((1,), (0,)))
                part += f32_dot(weighted[1][...], second[:, at : at + wide], ((1,), (0,)))
                grad[...] = part.astype(jnp.bfloat16)


def stack_kernel(flags, near, back, own, other):
    half, cols = near.shape[0], near.shape[1] // 2
    for z, (first, second) in enumerate(((near, back), (back, near))):

        @pl.when(flags[1] == z)
        def _(first=first, second=second):
            for at, out in enumerate((own, other)):
                out[:half, :] = first[:, at * cols : (at + 1) * cols]
                out[half:, :] = second[:, at * cols : (at + 1) * cols]


def output_kernel(count, *refs):
    flags, ups, downs = refs[0], refs[1 : count + 1], refs[count + 1 : 2 * count + 1]
    refs = refs[2 * count + 1 :]
    blocks, (gate, keep, send, whole) = refs[:-4], refs[-4:]
    place(flags, ups, whole)
    hidden = times_weight(whole, blocks) * gate[...].astype(jnp.float32)
    hidden = hidden.astype(jnp.bfloat16)
    place(flags, downs, whole)
    feats, wide = blocks[0].shape[1], whole.shape[2]
    per = count // len(blocks)
    for i in range(count):
        k = i // per
        at = (k >> 1) * feats + (i % per) * wide
        out = send if k & 1 else keep
        part = f32_dot(hidden, whole[i], ((0,), (0,)))
        out[:, at : at + wide] = part.astype(jnp.bfloat16)


class Plan:
    def __init__(self):
        self.steps, self.got, self.flying, self.token = {}, {}, {}, None

    def tie(self, values):
        values, self.token = lax.optimization_barrier((values, self.token))
        return values

    def exchange(self, name, axis, bit, source):
        def start():
            self.flying[name] = swap(self.tie(source()), axis, bit)

        def wait():
            self.got[name] = self.tie(self.flying.pop(name))

        self.steps["s " + name], self.steps["w " + name] = start, wait

    def compute(self, name, function, tied=True):
        def run():
            values = function()
            self.got[name] = self.tie(values) if tied else values

        self.steps["c " + name] = run

    def run(self, token, order):
        self.token = token
        steps = list(self.steps.values())
        if len(order) != len(steps):
            order = range(len(steps))
        for number in order:
            steps[number]()
        return self.got


def plan_pair(plan, name, first, order, turn):
    got = plan.got
    plan.compute("p" + name, first)
    plan.exchange(name + "_y", "dp", 0, lambda: got["p" + name][0])

    def pair():
        own, theirs = got["p" + name][1], got[name + "_y"]
        rows, cols = own.shape[::-1] if turn else own.shape
        out = bf16(rows // 2, 2 * cols)
        return pl.pallas_call(
            functools.partial(pair_kernel, turn),
            out_shape=(out, out),
            in_specs=[SMEM, VMEM, VMEM],
            out_specs=(VMEM, VMEM),
            compiler_params=SMALL,
            name="pair",
        )(scalars(bit_of("dp", 1), order), own, theirs)

    plan.compute("k" + name, pair)
    plan.exchange(name + "_zl", "dp", 1, lambda: got["k" + name][1])


def plan_weight(plan, name, first, nb):
    got = plan.got
    plan_pair(plan, name, first, bit_of("dp", 0), True)
    pieces = [lambda: got["k" + name][0], lambda: got[name + "_zl"]]
    for bit in range(2, nb):
        for piece in list(pieces):
            key = name + "_h" + str(len(pieces) - 2)
            plan.exchange(key, "dp", bit, piece)
            pieces.append(lambda key=key: got[key])
    return lambda: [piece() for piece in pieces]


def plan_tokens(plan, name, shard, nt):
    got, chunks = plan.got, {}
    plan.exchange(name + "b_zl", "dp", 1, lambda: shard)
    for chunk, own in (("a", lambda: shard), ("b", lambda: got[name + "b_zl"])):
        key = name + chunk
        plan.exchange(key + "_y", "dp", 0, own)
        plan.compute(
            "c" + key,
            lambda own=own, key=key: join(own(), got[key + "_y"]),
        )
        blocks = ["c" + key]
        for bit in range(nt - 1, -1, -1):
            new = []
            for index, block in enumerate(blocks):
                part = key + "_t" + str(bit) + str(index)
                plan.exchange(part, "tensor", bit, lambda block=block: got[block])
                new += [block, part]
            blocks = new
        chunks[chunk] = blocks
    return lambda chunk: [got[key] for key in chunks[chunk]]


def plan_collect(plan, name, near, away):
    got = plan.got
    y, z = bit_of("dp", 0), bit_of("dp", 1)
    plan.exchange(name + "_zl", "dp", 1, away)

    def stack():
        out = bf16(2 * near().shape[0], near().shape[1] // 2)
        return pl.pallas_call(
            stack_kernel,
            out_shape=(out, out),
            in_specs=[SMEM, VMEM, VMEM],
            out_specs=(VMEM, VMEM),
            compiler_params=SMALL,
            name="stack",
        )(scalars(y, z), near(), got[name + "_zl"])

    plan.compute("p" + name, stack)
    plan.exchange(name + "_y", "dp", 0, lambda: got["p" + name][1])

    def whole():
        own, theirs = got["p" + name][0], got[name + "_y"]
        return jnp.concatenate([pick(y, own, theirs), pick(y, theirs, own)], axis=0)

    return whole


def plan_scatter(plan, full, nb):
    got = plan.got
    y, z = bit_of("dp", 0), bit_of("dp", 1)
    half, number, pieces = 1 << (nb - 2), 0, []
    for index in range(2 * half):
        pieces.append(lambda index=index: full(index))
    for bit in range(nb - 1, 1, -1):
        half = len(pieces) // 2
        sums = []
        for index in reversed(range(half)):
            name = "R_h" + str(number)
            plan.exchange(name, "dp", bit, pieces[half + index])
            plan.compute(
                "a" + str(number),
                lambda mine=pieces[index], name=name: add_rounded(mine(), got[name])[0],
            )
            sums.insert(0, lambda key="a" + str(number): got[key])
            number += 1
        pieces = sums
    near, away = pieces
    plan.exchange("R_zl", "dp", 1, away)

    def rows():
        out = bf16(near().shape[1] // 2, 2 * near().shape[0])
        return pl.pallas_call(
            rows_kernel,
            out_shape=(out, out),
            in_specs=[SMEM, VMEM, VMEM],
            out_specs=(VMEM, VMEM),
            compiler_params=SMALL,
            name="rows",
        )(scalars(y, z), near(), got["R_zl"])

    plan.compute("ry", rows)
    plan.exchange("R_y", "dp", 0, lambda: got["ry"][1])

    def whole():
        own, theirs = got["ry"][0], got["R_y"]
        return jnp.concatenate([pick(y, own, theirs), pick(y, theirs, own)], axis=1)

    return whole


def plan_output(plan, part, tok, nt):
    got = plan.got
    for chunk in "ba":
        key = "O" + chunk
        plan.compute("kC" + chunk, lambda chunk=chunk: part(chunk))
        plan.exchange(key + "_t0", "tensor", 0, lambda chunk=chunk: got["kC" + chunk][1])
        last = "o0" + chunk
        plan.compute(
            last,
            lambda chunk=chunk, key=key: add_rounded(
                got["kC" + chunk][0], got[key + "_t0"], 2, int(nt > 1)
            ),
        )
        for bit in range(nt - 1, 0, -1):
            name, step = key + "_t" + str(bit), "o" + str(bit) + chunk
            plan.exchange(name, "tensor", bit, lambda last=last: got[last][1])
            plan.compute(
                step,
                lambda last=last, name=name, bit=bit: add_rounded(
                    got[last][0], got[name], 2, int(bit > 1)
                ),
            )
            last = step
        plan.exchange(key + "_y", "dp", 0, lambda last=last: got[last][1])
        plan.compute(
            "oy" + chunk,
            lambda last=last, key=key: add_rounded(got[last][0], got[key + "_y"])[0],
        )
        if chunk == "b":
            plan.exchange("O_zl", "dp", 1, lambda: got["oyb"])
    return lambda: add_rounded(got["oya"], got["O_zl"])[0]


def body(
    block_input, gate_act, grad_out, up_weight, down_weight, quant_step, round_logit, grid_offset
):
    n_dp, n_tensor = lax.axis_size("dp"), lax.axis_size("tensor")
    nb, nt = n_bits(n_dp), n_bits(n_tensor)
    tok, cols = gate_act.shape
    half, quarter = cols // 2, cols // 4
    rows = up_weight.shape[0]
    depth = rows * n_dp
    count = n_dp // 2
    y = bit_of("dp", 0)
    shift = (lax.axis_index("dp") >> 1) ^ (lax.axis_index("tensor") << (nb - 1 - nt))

    soft_bits = jax.nn.sigmoid(round_logit)
    centered = 2.0 * soft_bits - 1.0
    reg_local = jnp.sum(1.0 - (centered * centered) ** 2)

    def split(name, kernel, out, *operands):
        return pl.pallas_call(
            kernel,
            out_shape=(out, out),
            in_specs=[SMEM] + [VMEM] * len(operands),
            out_specs=(VMEM, VMEM),
            compiler_params=SMALL,
            name=name,
        )(scalars(y), *operands)

    plan = Plan()
    got = plan.got
    out = bf16(rows, half)
    down = plan_weight(plan, "D", lambda: split("split", split_kernel, out, down_weight.T), nb)
    grads = plan_tokens(plan, "G", grad_out, nt)
    plan_pair(
        plan, "g", lambda: split("split", half_kernel, bf16(half, tok), gate_act.T), 0, False
    )
    gate = lambda chunk: got["kg"][0] if chunk == "a" else got["g_zl"]
    delta = plan_weight(
        plan,
        "T",
        lambda: split(
            "delta", delta_kernel, out, round_logit, grid_offset, quant_step[None, :]
        ),
        nb,
    )
    features = plan_tokens(plan, "X", block_input, nt)
    up = plan_weight(plan, "U", lambda: split("split", split_kernel, out, up_weight), nb)
    whole = pltpu.VMEM((count, quarter, 2 * rows), jnp.bfloat16)

    def matmuls(name, kernel, out_shape, out_specs, *operands):
        return pl.pallas_call(
            functools.partial(kernel, count),
            out_shape=out_shape,
            in_specs=[SMEM] + [VMEM] * len(operands),
            out_specs=out_specs,
            scratch_shapes=[whole],
            compiler_params=PARAMS,
            name=name,
        )(scalars(shift), *operands)

    one = jax.ShapeDtypeStruct((1, 1), jnp.float32)
    for chunk in "ab":
        plan.compute(
            "kA" + chunk,
            lambda chunk=chunk: matmuls(
                "fisher_matmul",
                fisher_kernel,
                (bf16(quarter, 2 * tok), one),
                (VMEM, SMEM),
                *down(),
                *grads(chunk),
                gate(chunk),
            ),
        )
    fisher = lambda chunk: got["kA" + chunk][0]
    for chunk in "ab":
        plan.compute(
            "kR" + chunk,
            lambda chunk=chunk: matmuls(
                "residual_matmul",
                residual_kernel,
                (bf16(quarter, 2 * tok), one),
                (VMEM, SMEM),
                *delta(),
                *features(chunk),
                fisher(chunk),
            ),
        )

    def make_grad(wanted):
        operands = *features("a"), *features("b"), got["kRa"][0], got["kRb"][0]
        return pl.pallas_call(
            functools.partial(grad_kernel, count, wanted),
            out_shape=[bf16(quarter, 2 * rows)] * len(wanted),
            in_specs=[SMEM] + [VMEM] * len(operands),
            out_specs=[VMEM] * len(wanted),
            compiler_params=PARAMS,
            name="grad_matmul",
        )(scalars(shift), *operands)

    parts = [(j,) for j in reversed(range(count // 2, count))] + [tuple(range(count // 2))]
    where = {}
    for number, wanted in enumerate(parts):
        plan.compute("r" + str(number), lambda wanted=wanted: make_grad(wanted))
        for at, j in enumerate(wanted):
            where[j] = "r" + str(number), at
    grad_rows = plan_scatter(plan, lambda j: got[where[j][0]][where[j][1]], nb)
    fisher_rows = plan_collect(plan, "f", lambda: fisher("a"), lambda: fisher("b"))
    pair = bf16(2 * tok, depth // 2)
    out_rows = plan_output(
        plan,
        lambda chunk: matmuls(
            "output_matmul",
            output_kernel,
            (pair, pair),
            (VMEM, VMEM),
            *up(),
            *down(),
            *features(chunk),
            gate(chunk),
        ),
        tok,
        nt,
    )

    last = lambda: jnp.concatenate(
        [got["kAa"][1] + got["kAb"][1], got["kRa"][1] + got["kRb"][1], reg_local[None, None]], axis=1
    )
    for axis, bits in (("dp", nb), ("tensor", nt)):
        for bit in range(bits):
            name = "s_" + axis + str(bit)
            plan.exchange(name, axis, bit, last)
            plan.compute("q" + name, lambda last=last, name=name: last() + got[name], tied=False)
            last = lambda name=name: got["q" + name]

    plan.run(lax.axis_index("dp"), ORDER)

    sums = last()[0]
    fisher_sum, recon_total, reg_total = sums[0], sums[1], sums[2]
    total_cells = n_dp * n_tensor * tok * cols
    weight_cells = depth * n_tensor * cols
    fisher_mean = fisher_sum / total_cells
    sig_slope = soft_bits * (1.0 - soft_bits)
    grad_logit = (
        grad_rows().astype(jnp.float32)
        * (2.0 / fisher_mean)
        * quant_step[None, :]
        * sig_slope
        - reg_weight * 8.0 * centered**3 * sig_slope
    )
    loss = recon_total / (fisher_mean * total_cells) + reg_weight * reg_total / weight_cells
    loss = jnp.where(plan.token < 0, -loss, loss)
    return (out_rows(), fisher_rows().T, grad_logit, loss)


def solution(mesh):
    placed = (
        P("dp", "tensor"),
        P("dp", "tensor"),
        P("dp", "tensor"),
        P("dp", "tensor"),
        P("tensor", "dp"),
        P("tensor"),
        P("dp", "tensor"),
        P("dp", "tensor"),
    )
    return jax.shard_map(
        body,
        mesh=mesh,
        in_specs=placed,
        out_specs=(P("dp", "tensor"), P("dp", "tensor"), P("dp", "tensor"), P()),
        check_vma=False,
    )
```

```python
import functools

import jax
import jax.numpy as jnp
from jax import lax
from jax.experimental import pallas as pl
from jax.experimental.pallas import tpu as pltpu
from jax.sharding import PartitionSpec as P

reg_weight = 0.5

ORDER = (
    0,
    10,
    1,
    66,
    36,
    46,
    11,
    37,
    30,
    12,
    2,
    67,
    3,
    4,
    6,
    21,
    38,
    5,
    39,
    7,
    22,
    31,
    23,
    68,
    69,
    8,
    40,
    47,
    72,
    57,
    24,
    70,
    58,
    26,
    59,
    32,
    41,
    44,
    60,
    25,
    33,
    73,
    13,
    48,
    28,
    61,
    14,
    34,
    9,
    49,
    42,
    50,
    71,
    15,
    51,
    29,
    53,
    17,
    45,
    27,
    35,
    16,
    19,
    74,
    64,
    77,
    62,
    94,
    54,
    52,
    55,
    43,
    20,
    18,
    76,
    63,
    65,
    79,
    56,
    78,
    121,
    80,
    83,
    81,
    75,
    99,
    122,
    123,
    100,
    95,
    111,
    124,
    84,
    112,
    86,
    101,
    96,
    102,
    103,
    97,
    82,
    113,
    125,
    85,
    114,
    126,
    87,
    89,
    115,
    98,
    127,
    88,
    104,
    105,
    128,
    106,
    129,
    130,
    90,
    91,
    92,
    131,
    107,
    116,
    108,
    132,
    133,
    109,
    117,
    118,
    110,
    134,
    93,
    135,
    119,
    120,
)

VMEM = pl.BlockSpec(memory_space=pltpu.VMEM)
SMEM = pl.BlockSpec(memory_space=pltpu.SMEM)
ANY = pl.BlockSpec(memory_space=pl.ANY)
PARAMS = pltpu.CompilerParams(vmem_limit_bytes=22 * 1024 * 1024)
SMALL = pltpu.CompilerParams(vmem_limit_bytes=8 * 1024 * 1024)


def swap(values, axis, bit):
    pairs = [(i, i ^ (1 << bit)) for i in range(lax.axis_size(axis))]
    return lax.ppermute(values, axis, pairs)


def bit_of(axis, bit):
    return (lax.axis_index(axis) >> bit) & 1


def n_bits(size):
    return size.bit_length() - 1


def pick(flag, first, second):
    return jnp.where(flag == 0, first, second)


def f32_dot(left, right, dims):
    return lax.dot_general(left, right, (dims, ((), ())), preferred_element_type=jnp.float32)


def add_rounded(mine, theirs, parts=1, axis=0):
    shape = list(mine.shape)
    shape[axis] //= parts
    return pl.pallas_call(
        functools.partial(add_kernel, axis),
        out_shape=[bf16(*shape)] * parts,
        in_specs=[VMEM, VMEM],
        out_specs=[VMEM] * parts,
        compiler_params=SMALL,
        name="add",
    )(mine, theirs)


def join(first, second):
    return pl.pallas_call(
        join_kernel,
        out_shape=bf16(2 * first.shape[0], first.shape[1]),
        in_specs=[VMEM, VMEM],
        out_specs=VMEM,
        compiler_params=SMALL,
        name="join",
    )(first, second)


def scalars(*values):
    return jnp.stack([jnp.asarray(value, jnp.int32) for value in values])


def bf16(*shape):
    return jax.ShapeDtypeStruct(shape, jnp.bfloat16)


def store_halves(flag, values, send, keep, axis):
    half = values.shape[axis] // 2
    lower, upper = (values[:half], values[half:]) if axis == 0 else (values[:, :half], values[:, half:])

    @pl.when(flag == 0)
    def _():
        keep[...] = lower
        send[...] = upper

    @pl.when(flag != 0)
    def _():
        keep[...] = upper
        send[...] = lower


def split_kernel(flags, shard, send, keep):
    store_halves(flags[0], shard[...], send, keep, 1)


def delta_kernel(flags, logit, offset, step, send, keep):
    soft_bits = jax.nn.sigmoid(logit[...])
    delta = step[...] * (soft_bits - offset[...].astype(jnp.float32))
    store_halves(flags[0], delta.astype(jnp.bfloat16), send, keep, 1)


def half_kernel(flags, shard, send, keep):
    store_halves(flags[0], shard[...], send, keep, 0)


def pair_kernel(turn, flags, own, theirs, near, far):
    own, theirs = (own[...].T, theirs[...].T) if turn else (own[...], theirs[...])
    half, cols = own.shape[0] // 2, own.shape[1]
    for flag in (0, 1):

        @pl.when(flags[0] == flag)
        def _(flag=flag):
            for lower, out in ((0, near), (half, far)):
                start = half - lower if flag else lower
                for order, (left, right) in enumerate(((own, theirs), (theirs, own))):

                    @pl.when(flags[1] == order)
                    def _(start=start, out=out, left=left, right=right):
                        out[:, :cols] = left[start : start + half]
                        out[:, cols:] = right[start : start + half]


def join_kernel(first, second, out):
    rows = first.shape[0]
    out[:rows, :] = first[...]
    out[rows:, :] = second[...]


def add_kernel(axis, mine, theirs, *outs):
    total = mine[...].astype(jnp.float32) + theirs[...].astype(jnp.float32)
    total = total.astype(jnp.bfloat16)
    size = total.shape[axis] // len(outs)
    for i, out in enumerate(outs):
        at = slice(i * size, (i + 1) * size)
        out[...] = total[at] if axis == 0 else total[:, at]


def rows_kernel(flags, near, back, own, other):
    half, cols = near.shape[0], near.shape[1] // 2
    for z, (first, second) in enumerate(((near, back), (back, near))):

        @pl.when(flags[1] == z)
        def _(first=first, second=second):
            left = jnp.concatenate([first[:, :cols], second[:, :cols]], axis=0).T
            right = jnp.concatenate([first[:, cols:], second[:, cols:]], axis=0).T

            @pl.when(flags[0] == 0)
            def _():
                own[...] = left
                other[...] = right

            @pl.when(flags[0] != 0)
            def _():
                own[...] = right
                other[...] = left


def fetch(flags, pieces, blocks, whole, held, piece_sems, block_sems):
    copies = [
        pltpu.make_async_copy(piece, whole.at[j ^ flags[0]], piece_sems.at[j])
        for j, piece in enumerate(pieces)
    ]
    moved = [
        pltpu.make_async_copy(block, held.at[k], block_sems.at[k])
        for k, block in enumerate(blocks)
    ]
    for copy in copies + moved:
        copy.start()
    return copies, moved


def times_weight(whole, held, waits):
    count, _, wide = whole.shape
    per = count // held.shape[0]
    total = None
    for i in range(count):
        if i % per == 0:
            waits[i // per].wait()
        at = (i % per) * wide
        part = f32_dot(whole[i], held[i // per, :, at : at + wide], ((1,), (1,)))
        total = part if total is None else total + part
    return total


def fisher_kernel(count, *refs):
    flags, pieces, refs = refs[0], refs[1 : count + 1], refs[count + 1 :]
    blocks, (gate, fisher, total, *scratch) = refs[:-7], refs[-7:]
    whole, held = scratch[:2]
    copies, moved = fetch(flags, pieces, blocks, *scratch)
    for copy in copies:
        copy.wait()
    grads = times_weight(whole, held, moved)
    value = ((grads * gate[...].astype(jnp.float32)) ** 2).astype(jnp.bfloat16)
    fisher[...] = value
    total[0, 0] = jnp.sum(value.astype(jnp.float32))


def residual_kernel(count, *refs):
    flags, pieces, refs = refs[0], refs[1 : count + 1], refs[count + 1 :]
    blocks, (fisher, weighted, total, *scratch) = refs[:-7], refs[-7:]
    whole, held = scratch[:2]
    copies, moved = fetch(flags, pieces, blocks, *scratch)
    for copy in copies:
        copy.wait()
    residual = times_weight(whole, held, moved)
    value = fisher[...].astype(jnp.float32) * residual
    weighted[...] = value.astype(jnp.bfloat16)
    total[0, 0] = jnp.sum(value * residual)


def grad_kernel(count, wanted, flags, *refs):
    refs, (held, sems) = refs[:-2], refs[-2:]
    grads, refs = refs[-len(wanted) :], refs[: -len(wanted)]
    half = len(refs) // 2 - 1
    blocks, weighted = refs[: 2 * half], refs[2 * half :]
    wide = grads[0].shape[1]
    per = count // half

    def copies(number, i):
        return [
            pltpu.make_async_copy(
                blocks[chunk * half + i // per], held.at[2 * number + chunk], sems.at[2 * number + chunk]
            )
            for chunk in (0, 1)
        ]

    for number, j in enumerate(wanted):
        for i in range(count):

            @pl.when(flags[0] == i ^ j)
            def _(number=number, i=i):
                for copy in copies(number, i):
                    copy.start()

    for number, j in enumerate(wanted):
        for i in range(count):

            @pl.when(flags[0] == i ^ j)
            def _(number=number, i=i):
                at = (i % per) * wide
                first, second = copies(number, i)
                first.wait()
                part = f32_dot(weighted[0][...], held[2 * number, :, at : at + wide], ((1,), (0,)))
                second.wait()
                part += f32_dot(
                    weighted[1][...], held[2 * number + 1, :, at : at + wide], ((1,), (0,))
                )
                grads[number][...] = part.astype(jnp.bfloat16)


def stack_kernel(flags, near, back, own, other):
    half, cols = near.shape[0], near.shape[1] // 2
    for z, (first, second) in enumerate(((near, back), (back, near))):

        @pl.when(flags[1] == z)
        def _(first=first, second=second):
            for at, out in enumerate((own, other)):
                out[:half, :] = first[:, at * cols : (at + 1) * cols]
                out[half:, :] = second[:, at * cols : (at + 1) * cols]


def output_kernel(count, *refs):
    flags, ups, downs = refs[0], refs[1 : count + 1], refs[count + 1 : 2 * count + 1]
    refs = refs[2 * count + 1 :]
    blocks, (gate, keep, send, *scratch) = refs[:-8], refs[-8:]
    whole, held, back, sems, block_sems = scratch
    copies, moved = fetch(flags, ups, blocks, whole, held, sems.at[0], block_sems)
    later, _ = fetch(flags, downs, (), back, held, sems.at[1], block_sems)
    for copy in copies:
        copy.wait()
    hidden = times_weight(whole, held, moved) * gate[...].astype(jnp.float32)
    hidden = hidden.astype(jnp.bfloat16)
    for copy in later:
        copy.wait()
    feats, wide = held.shape[2], whole.shape[2]
    per = count // held.shape[0]
    for i in range(count):
        k = i // per
        at = (k >> 1) * feats + (i % per) * wide
        out = send if k & 1 else keep
        part = f32_dot(hidden, back[i], ((0,), (0,)))
        out[:, at : at + wide] = part.astype(jnp.bfloat16)


class Plan:
    def __init__(self):
        self.steps, self.got, self.flying, self.token = {}, {}, {}, None

    def tie(self, values):
        values, self.token = lax.optimization_barrier((values, self.token))
        return values

    def exchange(self, name, axis, bit, source):
        def start():
            self.flying[name] = swap(self.tie(source()), axis, bit)

        def wait():
            self.got[name] = self.tie(self.flying.pop(name))

        self.steps["s " + name], self.steps["w " + name] = start, wait

    def compute(self, name, function, tied=True):
        def run():
            values = function()
            self.got[name] = self.tie(values) if tied else values

        self.steps["c " + name] = run

    def run(self, token, order):
        self.token = token
        steps = list(self.steps.values())
        if len(order) != len(steps):
            order = range(len(steps))
        for number in order:
            steps[number]()
        return self.got


def plan_pair(plan, name, first, order, turn):
    got = plan.got
    plan.compute("p" + name, first)
    plan.exchange(name + "_y", "dp", 0, lambda: got["p" + name][0])

    def pair():
        own, theirs = got["p" + name][1], got[name + "_y"]
        rows, cols = own.shape[::-1] if turn else own.shape
        out = bf16(rows // 2, 2 * cols)
        return pl.pallas_call(
            functools.partial(pair_kernel, turn),
            out_shape=(out, out),
            in_specs=[SMEM, VMEM, VMEM],
            out_specs=(VMEM, VMEM),
            compiler_params=SMALL,
            name="pair",
        )(scalars(bit_of("dp", 1), order), own, theirs)

    plan.compute("k" + name, pair)
    plan.exchange(name + "_zl", "dp", 1, lambda: got["k" + name][1])


def plan_weight(plan, name, first, nb):
    got = plan.got
    plan_pair(plan, name, first, bit_of("dp", 0), True)
    pieces = [lambda: got["k" + name][0], lambda: got[name + "_zl"]]
    for bit in range(2, nb):
        for piece in list(pieces):
            key = name + "_h" + str(len(pieces) - 2)
            plan.exchange(key, "dp", bit, piece)
            pieces.append(lambda key=key: got[key])
    return lambda: [piece() for piece in pieces]


def plan_tokens(plan, name, shard, nt):
    got, chunks = plan.got, {}
    plan.exchange(name + "b_zl", "dp", 1, lambda: shard)
    for chunk, own in (("a", lambda: shard), ("b", lambda: got[name + "b_zl"])):
        key = name + chunk
        plan.exchange(key + "_y", "dp", 0, own)
        plan.compute(
            "c" + key,
            lambda own=own, key=key: join(own(), got[key + "_y"]),
        )
        blocks = ["c" + key]
        for bit in range(nt - 1, -1, -1):
            new = []
            for index, block in enumerate(blocks):
                part = key + "_t" + str(bit) + str(index)
                plan.exchange(part, "tensor", bit, lambda block=block: got[block])
                new += [block, part]
            blocks = new
        chunks[chunk] = blocks
    return lambda chunk: [got[key] for key in chunks[chunk]]


def plan_collect(plan, name, near, away):
    got = plan.got
    y, z = bit_of("dp", 0), bit_of("dp", 1)
    plan.exchange(name + "_zl", "dp", 1, away)

    def stack():
        out = bf16(2 * near().shape[0], near().shape[1] // 2)
        return pl.pallas_call(
            stack_kernel,
            out_shape=(out, out),
            in_specs=[SMEM, VMEM, VMEM],
            out_specs=(VMEM, VMEM),
            compiler_params=SMALL,
            name="stack",
        )(scalars(y, z), near(), got[name + "_zl"])

    plan.compute("p" + name, stack)
    plan.exchange(name + "_y", "dp", 0, lambda: got["p" + name][1])

    def whole():
        own, theirs = got["p" + name][0], got[name + "_y"]
        return jnp.concatenate([pick(y, own, theirs), pick(y, theirs, own)], axis=0)

    return whole


def plan_scatter(plan, full, nb):
    got = plan.got
    y, z = bit_of("dp", 0), bit_of("dp", 1)
    half, number, pieces = 1 << (nb - 2), 0, []
    for index in range(2 * half):
        pieces.append(lambda index=index: full(index))
    for bit in range(nb - 1, 1, -1):
        half = len(pieces) // 2
        sums = []
        for index in reversed(range(half)):
            name = "R_h" + str(number)
            plan.exchange(name, "dp", bit, pieces[half + index])
            plan.compute(
                "a" + str(number),
                lambda mine=pieces[index], name=name: add_rounded(mine(), got[name])[0],
            )
            sums.insert(0, lambda key="a" + str(number): got[key])
            number += 1
        pieces = sums
    near, away = pieces
    plan.exchange("R_zl", "dp", 1, away)

    def rows():
        out = bf16(near().shape[1] // 2, 2 * near().shape[0])
        return pl.pallas_call(
            rows_kernel,
            out_shape=(out, out),
            in_specs=[SMEM, VMEM, VMEM],
            out_specs=(VMEM, VMEM),
            compiler_params=SMALL,
            name="rows",
        )(scalars(y, z), near(), got["R_zl"])

    plan.compute("ry", rows)
    plan.exchange("R_y", "dp", 0, lambda: got["ry"][1])

    def whole():
        own, theirs = got["ry"][0], got["R_y"]
        return jnp.concatenate([pick(y, own, theirs), pick(y, theirs, own)], axis=1)

    return whole


def plan_output(plan, part, tok, nt):
    got = plan.got
    for chunk in "ba":
        key = "O" + chunk
        plan.compute("kC" + chunk, lambda chunk=chunk: part(chunk))
        plan.exchange(key + "_t0", "tensor", 0, lambda chunk=chunk: got["kC" + chunk][1])
        last = "o0" + chunk
        plan.compute(
            last,
            lambda chunk=chunk, key=key: add_rounded(
                got["kC" + chunk][0], got[key + "_t0"], 2, int(nt > 1)
            ),
        )
        for bit in range(nt - 1, 0, -1):
            name, step = key + "_t" + str(bit), "o" + str(bit) + chunk
            plan.exchange(name, "tensor", bit, lambda last=last: got[last][1])
            plan.compute(
                step,
                lambda last=last, name=name, bit=bit: add_rounded(
                    got[last][0], got[name], 2, int(bit > 1)
                ),
            )
            last = step
        plan.exchange(key + "_y", "dp", 0, lambda last=last: got[last][1])
        plan.compute(
            "oy" + chunk,
            lambda last=last, key=key: add_rounded(got[last][0], got[key + "_y"])[0],
        )
        if chunk == "b":
            plan.exchange("O_zl", "dp", 1, lambda: got["oyb"])
    return lambda: add_rounded(got["oya"], got["O_zl"])[0]


def body(
    block_input, gate_act, grad_out, up_weight, down_weight, quant_step, round_logit, grid_offset
):
    n_dp, n_tensor = lax.axis_size("dp"), lax.axis_size("tensor")
    nb, nt = n_bits(n_dp), n_bits(n_tensor)
    tok, cols = gate_act.shape
    half, quarter = cols // 2, cols // 4
    rows = up_weight.shape[0]
    feats = block_input.shape[1]
    depth = rows * n_dp
    count = n_dp // 2
    y = bit_of("dp", 0)
    shift = (lax.axis_index("dp") >> 1) ^ (lax.axis_index("tensor") << (nb - 1 - nt))

    soft_bits = jax.nn.sigmoid(round_logit)
    centered = 2.0 * soft_bits - 1.0
    reg_local = jnp.sum(1.0 - (centered * centered) ** 2)

    def split(name, kernel, out, *operands):
        return pl.pallas_call(
            kernel,
            out_shape=(out, out),
            in_specs=[SMEM] + [VMEM] * len(operands),
            out_specs=(VMEM, VMEM),
            compiler_params=SMALL,
            name=name,
        )(scalars(y), *operands)

    plan = Plan()
    got = plan.got
    out = bf16(rows, half)
    down = plan_weight(plan, "D", lambda: split("split", split_kernel, out, down_weight.T), nb)
    grads = plan_tokens(plan, "G", grad_out, nt)
    plan_pair(
        plan, "g", lambda: split("split", half_kernel, bf16(half, tok), gate_act.T), 0, False
    )
    gate = lambda chunk: got["kg"][0] if chunk == "a" else got["g_zl"]
    delta = plan_weight(
        plan,
        "T",
        lambda: split(
            "delta", delta_kernel, out, round_logit, grid_offset, quant_step[None, :]
        ),
        nb,
    )
    features = plan_tokens(plan, "X", block_input, nt)
    up = plan_weight(plan, "U", lambda: split("split", split_kernel, out, up_weight), nb)
    whole = pltpu.VMEM((count, quarter, 2 * rows), jnp.bfloat16)
    held = pltpu.VMEM((n_tensor, 2 * tok, feats), jnp.bfloat16)
    sems = pltpu.SemaphoreType.DMA

    def matmuls(name, kernel, out_shape, out_specs, scratch, *operands):
        return pl.pallas_call(
            functools.partial(kernel, count),
            out_shape=out_shape,
            in_specs=[SMEM] + [ANY] * (len(operands) - 1) + [VMEM],
            out_specs=out_specs,
            scratch_shapes=scratch,
            compiler_params=PARAMS,
            name=name,
        )(scalars(shift), *operands)

    simple = [whole, held, sems((count,)), sems((n_tensor,))]
    one = jax.ShapeDtypeStruct((1, 1), jnp.float32)
    for chunk in "ab":
        plan.compute(
            "kA" + chunk,
            lambda chunk=chunk: matmuls(
                "fisher_matmul",
                fisher_kernel,
                (bf16(quarter, 2 * tok), one),
                (VMEM, SMEM),
                simple,
                *down(),
                *grads(chunk),
                gate(chunk),
            ),
        )
    fisher = lambda chunk: got["kA" + chunk][0]
    for chunk in "ab":
        plan.compute(
            "kR" + chunk,
            lambda chunk=chunk: matmuls(
                "residual_matmul",
                residual_kernel,
                (bf16(quarter, 2 * tok), one),
                (VMEM, SMEM),
                simple,
                *delta(),
                *features(chunk),
                fisher(chunk),
            ),
        )

    def make_grad(wanted):
        operands = *features("a"), *features("b"), got["kRa"][0], got["kRb"][0]
        return pl.pallas_call(
            functools.partial(grad_kernel, count, wanted),
            out_shape=[bf16(quarter, 2 * rows)] * len(wanted),
            in_specs=[SMEM] + [ANY] * (len(operands) - 2) + [VMEM, VMEM],
            out_specs=[VMEM] * len(wanted),
            scratch_shapes=[
                pltpu.VMEM((2 * len(wanted), 2 * tok, feats), jnp.bfloat16),
                sems((2 * len(wanted),)),
            ],
            compiler_params=PARAMS,
            name="grad_matmul",
        )(scalars(shift), *operands)

    parts = [(j,) for j in reversed(range(count // 2, count))] + [tuple(range(count // 2))]
    where = {}
    for number, wanted in enumerate(parts):
        plan.compute("r" + str(number), lambda wanted=wanted: make_grad(wanted))
        for at, j in enumerate(wanted):
            where[j] = "r" + str(number), at
    grad_rows = plan_scatter(plan, lambda j: got[where[j][0]][where[j][1]], nb)
    fisher_rows = plan_collect(plan, "f", lambda: fisher("a"), lambda: fisher("b"))
    pair = bf16(2 * tok, depth // 2)
    out_rows = plan_output(
        plan,
        lambda chunk: matmuls(
            "output_matmul",
            output_kernel,
            (pair, pair),
            (VMEM, VMEM),
            [whole, held, whole, sems((2, count)), sems((n_tensor,))],
            *up(),
            *down(),
            *features(chunk),
            gate(chunk),
        ),
        tok,
        nt,
    )

    last = lambda: jnp.concatenate(
        [got["kAa"][1] + got["kAb"][1], got["kRa"][1] + got["kRb"][1], reg_local[None, None]], axis=1
    )
    for axis, bits in (("dp", nb), ("tensor", nt)):
        for bit in range(bits):
            name = "s_" + axis + str(bit)
            plan.exchange(name, axis, bit, last)
            plan.compute("q" + name, lambda last=last, name=name: last() + got[name], tied=False)
            last = lambda name=name: got["q" + name]

    plan.run(lax.axis_index("dp"), ORDER)

    sums = last()[0]
    fisher_sum, recon_total, reg_total = sums[0], sums[1], sums[2]
    total_cells = n_dp * n_tensor * tok * cols
    weight_cells = depth * n_tensor * cols
    fisher_mean = fisher_sum / total_cells
    sig_slope = soft_bits * (1.0 - soft_bits)
    grad_logit = (
        grad_rows().astype(jnp.float32)
        * (2.0 / fisher_mean)
        * quant_step[None, :]
        * sig_slope
        - reg_weight * 8.0 * centered**3 * sig_slope
    )
    loss = recon_total / (fisher_mean * total_cells) + reg_weight * reg_total / weight_cells
    loss = jnp.where(plan.token < 0, -loss, loss)
    return (out_rows(), fisher_rows().T, grad_logit, loss)


def solution(mesh):
    placed = (
        P("dp", "tensor"),
        P("dp", "tensor"),
        P("dp", "tensor"),
        P("dp", "tensor"),
        P("tensor", "dp"),
        P("tensor"),
        P("dp", "tensor"),
        P("dp", "tensor"),
    )
    return jax.shard_map(
        body,
        mesh=mesh,
        in_specs=placed,
        out_specs=(P("dp", "tensor"), P("dp", "tensor"), P("dp", "tensor"), P()),
        check_vma=False,
    )
```

```python
import functools

import jax
import jax.numpy as jnp
from jax import lax
from jax.experimental import pallas as pl
from jax.experimental.pallas import tpu as pltpu
from jax.sharding import PartitionSpec as P

reg_weight = 0.5

ORDER = (
    46,
    0,
    12,
    1,
    66,
    36,
    30,
    67,
    47,
    10,
    2,
    3,
    57,
    37,
    6,
    11,
    4,
    68,
    69,
    21,
    38,
    39,
    40,
    7,
    72,
    48,
    70,
    5,
    22,
    23,
    8,
    24,
    13,
    73,
    58,
    41,
    31,
    14,
    59,
    25,
    26,
    60,
    32,
    15,
    44,
    71,
    33,
    42,
    28,
    9,
    49,
    62,
    34,
    50,
    61,
    16,
    64,
    51,
    74,
    45,
    17,
    27,
    35,
    29,
    19,
    77,
    52,
    53,
    65,
    43,
    55,
    94,
    18,
    20,
    54,
    63,
    76,
    56,
    78,
    79,
    80,
    121,
    83,
    81,
    75,
    99,
    122,
    100,
    95,
    111,
    84,
    112,
    101,
    102,
    103,
    123,
    86,
    124,
    82,
    113,
    125,
    96,
    114,
    97,
    115,
    85,
    89,
    126,
    87,
    104,
    105,
    106,
    127,
    88,
    128,
    90,
    98,
    91,
    92,
    129,
    130,
    116,
    107,
    117,
    131,
    132,
    108,
    118,
    133,
    109,
    93,
    134,
    135,
    110,
    119,
    120,
)

VMEM = pl.BlockSpec(memory_space=pltpu.VMEM)
SMEM = pl.BlockSpec(memory_space=pltpu.SMEM)
ANY = pl.BlockSpec(memory_space=pl.ANY)
PARAMS = pltpu.CompilerParams(vmem_limit_bytes=20 * 1024 * 1024)
SMALL = pltpu.CompilerParams(vmem_limit_bytes=20 * 1024 * 1024)


def swap(values, axis, bit):
    pairs = [(i, i ^ (1 << bit)) for i in range(lax.axis_size(axis))]
    return lax.ppermute(values, axis, pairs)


def bit_of(axis, bit):
    return (lax.axis_index(axis) >> bit) & 1


def n_bits(size):
    return size.bit_length() - 1


def pick(flag, first, second):
    return jnp.where(flag == 0, first, second)


def f32_dot(left, right, dims):
    return lax.dot_general(left, right, (dims, ((), ())), preferred_element_type=jnp.float32)


def add_rounded(mine, theirs, parts=1, axis=0):
    shape = list(mine.shape)
    shape[axis] //= parts
    return pl.pallas_call(
        functools.partial(add_kernel, axis),
        out_shape=[bf16(*shape)] * parts,
        in_specs=[VMEM, VMEM],
        out_specs=[VMEM] * parts,
        compiler_params=SMALL,
        name="add",
    )(mine, theirs)


def join(first, second):
    return pl.pallas_call(
        join_kernel,
        out_shape=bf16(2 * first.shape[0], first.shape[1]),
        in_specs=[VMEM, VMEM],
        out_specs=VMEM,
        compiler_params=SMALL,
        name="join",
    )(first, second)


def scalars(*values):
    return jnp.stack([jnp.asarray(value, jnp.int32) for value in values])


def bf16(*shape):
    return jax.ShapeDtypeStruct(shape, jnp.bfloat16)


def store_halves(flag, values, send, keep, axis):
    half = values.shape[axis] // 2
    lower, upper = (values[:half], values[half:]) if axis == 0 else (values[:, :half], values[:, half:])

    @pl.when(flag == 0)
    def _():
        keep[...] = lower
        send[...] = upper

    @pl.when(flag != 0)
    def _():
        keep[...] = upper
        send[...] = lower


def split_kernel(flags, shard, send, keep):
    store_halves(flags[0], shard[...], send, keep, 1)


def delta_kernel(flags, logit, offset, step, send, keep):
    soft_bits = jax.nn.sigmoid(logit[...])
    delta = step[...] * (soft_bits - offset[...].astype(jnp.float32))
    store_halves(flags[0], delta.astype(jnp.bfloat16), send, keep, 1)


def half_kernel(flags, shard, send, keep):
    store_halves(flags[0], shard[...], send, keep, 0)


def pair_kernel(turn, flags, own, theirs, near, far):
    own, theirs = (own[...].T, theirs[...].T) if turn else (own[...], theirs[...])
    half, cols = own.shape[0] // 2, own.shape[1]
    for flag in (0, 1):

        @pl.when(flags[0] == flag)
        def _(flag=flag):
            for lower, out in ((0, near), (half, far)):
                start = half - lower if flag else lower
                for order, (left, right) in enumerate(((own, theirs), (theirs, own))):

                    @pl.when(flags[1] == order)
                    def _(start=start, out=out, left=left, right=right):
                        out[:, :cols] = left[start : start + half]
                        out[:, cols:] = right[start : start + half]


def join_kernel(first, second, out):
    rows = first.shape[0]
    out[:rows, :] = first[...]
    out[rows:, :] = second[...]


def add_kernel(axis, mine, theirs, *outs):
    total = mine[...].astype(jnp.float32) + theirs[...].astype(jnp.float32)
    total = total.astype(jnp.bfloat16)
    size = total.shape[axis] // len(outs)
    for i, out in enumerate(outs):
        at = slice(i * size, (i + 1) * size)
        out[...] = total[at] if axis == 0 else total[:, at]


def rows_kernel(flags, near, back, own, other):
    half, cols = near.shape[0], near.shape[1] // 2
    for z, (first, second) in enumerate(((near, back), (back, near))):

        @pl.when(flags[1] == z)
        def _(first=first, second=second):
            left = jnp.concatenate([first[:, :cols], second[:, :cols]], axis=0).T
            right = jnp.concatenate([first[:, cols:], second[:, cols:]], axis=0).T

            @pl.when(flags[0] == 0)
            def _():
                own[...] = left
                other[...] = right

            @pl.when(flags[0] != 0)
            def _():
                own[...] = right
                other[...] = left


def fetch(flags, pieces, blocks, whole, held, piece_sems, block_sems):
    copies = [
        pltpu.make_async_copy(piece, whole.at[j ^ flags[0]], piece_sems.at[j])
        for j, piece in enumerate(pieces)
    ]
    moved = [
        pltpu.make_async_copy(block, held.at[k], block_sems.at[k])
        for k, block in enumerate(blocks)
    ]
    for copy in copies + moved:
        copy.start()
    return copies, moved


def times_weight(whole, held, waits):
    count, _, wide = whole.shape
    per = count // held.shape[0]
    total = None
    for i in range(count):
        if i % per == 0:
            waits[i // per].wait()
        at = (i % per) * wide
        part = f32_dot(whole[i], held[i // per, :, at : at + wide], ((1,), (1,)))
        total = part if total is None else total + part
    return total


def fisher_kernel(count, *refs):
    flags, pieces, refs = refs[0], refs[1 : count + 1], refs[count + 1 :]
    blocks, (gate, fisher, total, *scratch) = refs[:-7], refs[-7:]
    whole, held = scratch[:2]
    copies, moved = fetch(flags, pieces, blocks, *scratch)
    for copy in copies:
        copy.wait()
    grads = times_weight(whole, held, moved)
    value = ((grads * gate[...].astype(jnp.float32)) ** 2).astype(jnp.bfloat16)
    fisher[...] = value
    total[0, 0] = jnp.sum(value.astype(jnp.float32))


def residual_kernel(count, *refs):
    flags, pieces, refs = refs[0], refs[1 : count + 1], refs[count + 1 :]
    blocks, (fisher, weighted, total, *scratch) = refs[:-7], refs[-7:]
    whole, held = scratch[:2]
    copies, moved = fetch(flags, pieces, blocks, *scratch)
    for copy in copies:
        copy.wait()
    residual = times_weight(whole, held, moved)
    value = fisher[...].astype(jnp.float32) * residual
    weighted[...] = value.astype(jnp.bfloat16)
    total[0, 0] = jnp.sum(value * residual)


def grad_kernel(count, wanted, flags, *refs):
    refs, (held, sems) = refs[:-2], refs[-2:]
    grads, refs = refs[-len(wanted) :], refs[: -len(wanted)]
    half = len(refs) // 2 - 1
    blocks, weighted = refs[: 2 * half], refs[2 * half :]
    wide = grads[0].shape[1]
    per = count // half

    def copies(number, i):
        return [
            pltpu.make_async_copy(
                blocks[chunk * half + i // per], held.at[2 * number + chunk], sems.at[2 * number + chunk]
            )
            for chunk in (0, 1)
        ]

    for number, j in enumerate(wanted):
        for i in range(count):

            @pl.when(flags[0] == i ^ j)
            def _(number=number, i=i):
                for copy in copies(number, i):
                    copy.start()

    for number, j in enumerate(wanted):
        for i in range(count):

            @pl.when(flags[0] == i ^ j)
            def _(number=number, i=i):
                at = (i % per) * wide
                first, second = copies(number, i)
                first.wait()
                part = f32_dot(weighted[0][...], held[2 * number, :, at : at + wide], ((1,), (0,)))
                second.wait()
                part += f32_dot(
                    weighted[1][...], held[2 * number + 1, :, at : at + wide], ((1,), (0,))
                )
                grads[number][...] = part.astype(jnp.bfloat16)


def stack_kernel(flags, near, back, own, other):
    half, cols = near.shape[0], near.shape[1] // 2
    for z, (first, second) in enumerate(((near, back), (back, near))):

        @pl.when(flags[1] == z)
        def _(first=first, second=second):
            for at, out in enumerate((own, other)):
                out[:half, :] = first[:, at * cols : (at + 1) * cols]
                out[half:, :] = second[:, at * cols : (at + 1) * cols]


def output_kernel(count, *refs):
    flags, ups, downs = refs[0], refs[1 : count + 1], refs[count + 1 : 2 * count + 1]
    refs = refs[2 * count + 1 :]
    blocks, (gate, keep, send, *scratch) = refs[:-8], refs[-8:]
    whole, held, back, sems, block_sems = scratch
    copies, moved = fetch(flags, ups, blocks, whole, held, sems.at[0], block_sems)
    later, _ = fetch(flags, downs, (), back, held, sems.at[1], block_sems)
    for copy in copies:
        copy.wait()
    hidden = times_weight(whole, held, moved) * gate[...].astype(jnp.float32)
    hidden = hidden.astype(jnp.bfloat16)
    for copy in later:
        copy.wait()
    feats, wide = held.shape[2], whole.shape[2]
    per = count // held.shape[0]
    for i in range(count):
        k = i // per
        at = (k >> 1) * feats + (i % per) * wide
        out = send if k & 1 else keep
        part = f32_dot(hidden, back[i], ((0,), (0,)))
        out[:, at : at + wide] = part.astype(jnp.bfloat16)


class Plan:
    def __init__(self):
        self.steps, self.got, self.flying, self.token = {}, {}, {}, None

    def tie(self, values):
        values, self.token = lax.optimization_barrier((values, self.token))
        return values

    def exchange(self, name, axis, bit, source):
        def start():
            self.flying[name] = swap(self.tie(source()), axis, bit)

        def wait():
            self.got[name] = self.tie(self.flying.pop(name))

        self.steps["s " + name], self.steps["w " + name] = start, wait

    def compute(self, name, function, tied=True):
        def run():
            values = function()
            self.got[name] = self.tie(values) if tied else values

        self.steps["c " + name] = run

    def run(self, token, order):
        self.token = token
        steps = list(self.steps.values())
        if len(order) != len(steps):
            order = range(len(steps))
        for number in order:
            steps[number]()
        return self.got


def plan_pair(plan, name, first, order, turn):
    got = plan.got
    plan.compute("p" + name, first)
    plan.exchange(name + "_y", "dp", 0, lambda: got["p" + name][0])

    def pair():
        own, theirs = got["p" + name][1], got[name + "_y"]
        rows, cols = own.shape[::-1] if turn else own.shape
        out = bf16(rows // 2, 2 * cols)
        return pl.pallas_call(
            functools.partial(pair_kernel, turn),
            out_shape=(out, out),
            in_specs=[SMEM, VMEM, VMEM],
            out_specs=(VMEM, VMEM),
            compiler_params=SMALL,
            name="pair",
        )(scalars(bit_of("dp", 1), order), own, theirs)

    plan.compute("k" + name, pair)
    plan.exchange(name + "_zl", "dp", 1, lambda: got["k" + name][1])


def plan_weight(plan, name, first, nb):
    got = plan.got
    plan_pair(plan, name, first, bit_of("dp", 0), True)
    pieces = [lambda: got["k" + name][0], lambda: got[name + "_zl"]]
    for bit in range(2, nb):
        for piece in list(pieces):
            key = name + "_h" + str(len(pieces) - 2)
            plan.exchange(key, "dp", bit, piece)
            pieces.append(lambda key=key: got[key])
    return lambda: [piece() for piece in pieces]


def plan_tokens(plan, name, shard, nt):
    got, chunks = plan.got, {}
    plan.exchange(name + "b_zl", "dp", 1, lambda: shard)
    for chunk, own in (("a", lambda: shard), ("b", lambda: got[name + "b_zl"])):
        key = name + chunk
        plan.exchange(key + "_y", "dp", 0, own)
        plan.compute(
            "c" + key,
            lambda own=own, key=key: join(own(), got[key + "_y"]),
        )
        blocks = ["c" + key]
        for bit in range(nt - 1, -1, -1):
            new = []
            for index, block in enumerate(blocks):
                part = key + "_t" + str(bit) + str(index)
                plan.exchange(part, "tensor", bit, lambda block=block: got[block])
                new += [block, part]
            blocks = new
        chunks[chunk] = blocks
    return lambda chunk: [got[key] for key in chunks[chunk]]


def plan_collect(plan, name, near, away):
    got = plan.got
    y, z = bit_of("dp", 0), bit_of("dp", 1)
    plan.exchange(name + "_zl", "dp", 1, away)

    def stack():
        out = bf16(2 * near().shape[0], near().shape[1] // 2)
        return pl.pallas_call(
            stack_kernel,
            out_shape=(out, out),
            in_specs=[SMEM, VMEM, VMEM],
            out_specs=(VMEM, VMEM),
            compiler_params=SMALL,
            name="stack",
        )(scalars(y, z), near(), got[name + "_zl"])

    plan.compute("p" + name, stack)
    plan.exchange(name + "_y", "dp", 0, lambda: got["p" + name][1])

    def whole():
        own, theirs = got["p" + name][0], got[name + "_y"]
        return jnp.concatenate([pick(y, own, theirs), pick(y, theirs, own)], axis=0)

    return whole


def plan_scatter(plan, full, nb):
    got = plan.got
    y, z = bit_of("dp", 0), bit_of("dp", 1)
    half, number, pieces = 1 << (nb - 2), 0, []
    for index in range(2 * half):
        pieces.append(lambda index=index: full(index))
    for bit in range(nb - 1, 1, -1):
        half = len(pieces) // 2
        sums = []
        for index in reversed(range(half)):
            name = "R_h" + str(number)
            plan.exchange(name, "dp", bit, pieces[half + index])
            plan.compute(
                "a" + str(number),
                lambda mine=pieces[index], name=name: add_rounded(mine(), got[name])[0],
            )
            sums.insert(0, lambda key="a" + str(number): got[key])
            number += 1
        pieces = sums
    near, away = pieces
    plan.exchange("R_zl", "dp", 1, away)

    def rows():
        out = bf16(near().shape[1] // 2, 2 * near().shape[0])
        return pl.pallas_call(
            rows_kernel,
            out_shape=(out, out),
            in_specs=[SMEM, VMEM, VMEM],
            out_specs=(VMEM, VMEM),
            compiler_params=SMALL,
            name="rows",
        )(scalars(y, z), near(), got["R_zl"])

    plan.compute("ry", rows)
    plan.exchange("R_y", "dp", 0, lambda: got["ry"][1])

    def whole():
        own, theirs = got["ry"][0], got["R_y"]
        return jnp.concatenate([pick(y, own, theirs), pick(y, theirs, own)], axis=1)

    return whole


def plan_output(plan, part, tok, nt):
    got = plan.got
    for chunk in "ba":
        key = "O" + chunk
        plan.compute("kC" + chunk, lambda chunk=chunk: part(chunk))
        plan.exchange(key + "_t0", "tensor", 0, lambda chunk=chunk: got["kC" + chunk][1])
        last = "o0" + chunk
        plan.compute(
            last,
            lambda chunk=chunk, key=key: add_rounded(
                got["kC" + chunk][0], got[key + "_t0"], 2, int(nt > 1)
            ),
        )
        for bit in range(nt - 1, 0, -1):
            name, step = key + "_t" + str(bit), "o" + str(bit) + chunk
            plan.exchange(name, "tensor", bit, lambda last=last: got[last][1])
            plan.compute(
                step,
                lambda last=last, name=name, bit=bit: add_rounded(
                    got[last][0], got[name], 2, int(bit > 1)
                ),
            )
            last = step
        plan.exchange(key + "_y", "dp", 0, lambda last=last: got[last][1])
        plan.compute(
            "oy" + chunk,
            lambda last=last, key=key: add_rounded(got[last][0], got[key + "_y"])[0],
        )
        if chunk == "b":
            plan.exchange("O_zl", "dp", 1, lambda: got["oyb"])
    return lambda: add_rounded(got["oya"], got["O_zl"])[0]


def body(
    block_input, gate_act, grad_out, up_weight, down_weight, quant_step, round_logit, grid_offset
):
    n_dp, n_tensor = lax.axis_size("dp"), lax.axis_size("tensor")
    nb, nt = n_bits(n_dp), n_bits(n_tensor)
    tok, cols = gate_act.shape
    half, quarter = cols // 2, cols // 4
    rows = up_weight.shape[0]
    feats = block_input.shape[1]
    depth = rows * n_dp
    count = n_dp // 2
    y = bit_of("dp", 0)
    shift = (lax.axis_index("dp") >> 1) ^ (lax.axis_index("tensor") << (nb - 1 - nt))

    soft_bits = jax.nn.sigmoid(round_logit)
    centered = 2.0 * soft_bits - 1.0
    reg_local = jnp.sum(1.0 - (centered * centered) ** 2)

    def split(name, kernel, out, *operands):
        return pl.pallas_call(
            kernel,
            out_shape=(out, out),
            in_specs=[SMEM] + [VMEM] * len(operands),
            out_specs=(VMEM, VMEM),
            compiler_params=SMALL,
            name=name,
        )(scalars(y), *operands)

    plan = Plan()
    got = plan.got
    out = bf16(rows, half)
    down = plan_weight(plan, "D", lambda: split("split", split_kernel, out, down_weight.T), nb)
    grads = plan_tokens(plan, "G", grad_out, nt)
    plan_pair(
        plan, "g", lambda: split("split", half_kernel, bf16(half, tok), gate_act.T), 0, False
    )
    gate = lambda chunk: got["kg"][0] if chunk == "a" else got["g_zl"]
    delta = plan_weight(
        plan,
        "T",
        lambda: split(
            "delta", delta_kernel, out, round_logit, grid_offset, quant_step[None, :]
        ),
        nb,
    )
    features = plan_tokens(plan, "X", block_input, nt)
    up = plan_weight(plan, "U", lambda: split("split", split_kernel, out, up_weight), nb)
    whole = pltpu.VMEM((count, quarter, 2 * rows), jnp.bfloat16)
    held = pltpu.VMEM((n_tensor, 2 * tok, feats), jnp.bfloat16)
    sems = pltpu.SemaphoreType.DMA

    def matmuls(name, kernel, out_shape, out_specs, scratch, *operands):
        return pl.pallas_call(
            functools.partial(kernel, count),
            out_shape=out_shape,
            in_specs=[SMEM] + [ANY] * (len(operands) - 1) + [VMEM],
            out_specs=out_specs,
            scratch_shapes=scratch,
            compiler_params=PARAMS,
            name=name,
        )(scalars(shift), *operands)

    simple = [whole, held, sems((count,)), sems((n_tensor,))]
    one = jax.ShapeDtypeStruct((1, 1), jnp.float32)
    for chunk in "ab":
        plan.compute(
            "kA" + chunk,
            lambda chunk=chunk: matmuls(
                "fisher_matmul",
                fisher_kernel,
                (bf16(quarter, 2 * tok), one),
                (VMEM, SMEM),
                simple,
                *down(),
                *grads(chunk),
                gate(chunk),
            ),
        )
    fisher = lambda chunk: got["kA" + chunk][0]
    for chunk in "ab":
        plan.compute(
            "kR" + chunk,
            lambda chunk=chunk: matmuls(
                "residual_matmul",
                residual_kernel,
                (bf16(quarter, 2 * tok), one),
                (VMEM, SMEM),
                simple,
                *delta(),
                *features(chunk),
                fisher(chunk),
            ),
        )

    def make_grad(wanted):
        operands = *features("a"), *features("b"), got["kRa"][0], got["kRb"][0]
        return pl.pallas_call(
            functools.partial(grad_kernel, count, wanted),
            out_shape=[bf16(quarter, 2 * rows)] * len(wanted),
            in_specs=[SMEM] + [ANY] * (len(operands) - 2) + [VMEM, VMEM],
            out_specs=[VMEM] * len(wanted),
            scratch_shapes=[
                pltpu.VMEM((2 * len(wanted), 2 * tok, feats), jnp.bfloat16),
                sems((2 * len(wanted),)),
            ],
            compiler_params=PARAMS,
            name="grad_matmul",
        )(scalars(shift), *operands)

    parts = [(j,) for j in reversed(range(count // 2, count))] + [tuple(range(count // 2))]
    where = {}
    for number, wanted in enumerate(parts):
        plan.compute("r" + str(number), lambda wanted=wanted: make_grad(wanted))
        for at, j in enumerate(wanted):
            where[j] = "r" + str(number), at
    grad_rows = plan_scatter(plan, lambda j: got[where[j][0]][where[j][1]], nb)
    fisher_rows = plan_collect(plan, "f", lambda: fisher("a"), lambda: fisher("b"))
    pair = bf16(2 * tok, depth // 2)
    out_rows = plan_output(
        plan,
        lambda chunk: matmuls(
            "output_matmul",
            output_kernel,
            (pair, pair),
            (VMEM, VMEM),
            [whole, held, whole, sems((2, count)), sems((n_tensor,))],
            *up(),
            *down(),
            *features(chunk),
            gate(chunk),
        ),
        tok,
        nt,
    )

    last = lambda: jnp.concatenate(
        [got["kAa"][1] + got["kAb"][1], got["kRa"][1] + got["kRb"][1], reg_local[None, None]], axis=1
    )
    for axis, bits in (("dp", nb), ("tensor", nt)):
        for bit in range(bits):
            name = "s_" + axis + str(bit)
            plan.exchange(name, axis, bit, last)
            plan.compute("q" + name, lambda last=last, name=name: last() + got[name], tied=False)
            last = lambda name=name: got["q" + name]

    plan.run(lax.axis_index("dp"), ORDER)

    sums = last()[0]
    fisher_sum, recon_total, reg_total = sums[0], sums[1], sums[2]
    total_cells = n_dp * n_tensor * tok * cols
    weight_cells = depth * n_tensor * cols
    fisher_mean = fisher_sum / total_cells
    sig_slope = soft_bits * (1.0 - soft_bits)
    grad_logit = (
        grad_rows().astype(jnp.float32)
        * (2.0 / fisher_mean)
        * quant_step[None, :]
        * sig_slope
        - reg_weight * 8.0 * centered**3 * sig_slope
    )
    loss = recon_total / (fisher_mean * total_cells) + reg_weight * reg_total / weight_cells
    loss = jnp.where(plan.token < 0, -loss, loss)
    return (out_rows(), fisher_rows().T, grad_logit, loss)


def solution(mesh):
    placed = (
        P("dp", "tensor"),
        P("dp", "tensor"),
        P("dp", "tensor"),
        P("dp", "tensor"),
        P("tensor", "dp"),
        P("tensor"),
        P("dp", "tensor"),
        P("dp", "tensor"),
    )
    return jax.shard_map(
        body,
        mesh=mesh,
        in_specs=placed,
        out_specs=(P("dp", "tensor"), P("dp", "tensor"), P("dp", "tensor"), P()),
        check_vma=False,
    )
```

```python
import functools

import jax
import jax.numpy as jnp
from jax import lax
from jax.experimental import pallas as pl
from jax.experimental.pallas import tpu as pltpu
from jax.sharding import PartitionSpec as P

reg_weight = 0.5

ORDER = (
    46,
    0,
    1,
    66,
    67,
    36,
    10,
    47,
    30,
    37,
    12,
    57,
    2,
    3,
    4,
    6,
    11,
    58,
    48,
    68,
    69,
    70,
    72,
    7,
    59,
    60,
    49,
    13,
    5,
    31,
    14,
    15,
    8,
    50,
    53,
    51,
    73,
    32,
    33,
    34,
    71,
    61,
    74,
    21,
    17,
    9,
    38,
    64,
    39,
    62,
    52,
    42,
    55,
    22,
    23,
    75,
    16,
    19,
    35,
    56,
    63,
    18,
    24,
    40,
    26,
    54,
    65,
    99,
    100,
    111,
    112,
    43,
    41,
    27,
    20,
    44,
    25,
    28,
    76,
    113,
    29,
    101,
    102,
    103,
    114,
    115,
    77,
    94,
    45,
    78,
    79,
    121,
    80,
    83,
    82,
    122,
    123,
    95,
    124,
    96,
    125,
    104,
    105,
    106,
    116,
    97,
    117,
    81,
    86,
    118,
    84,
    85,
    89,
    107,
    126,
    127,
    108,
    109,
    87,
    88,
    90,
    91,
    128,
    92,
    129,
    130,
    131,
    132,
    133,
    119,
    120,
    134,
    135,
    110,
    98,
    93,
)

VMEM = pl.BlockSpec(memory_space=pltpu.VMEM)
SMEM = pl.BlockSpec(memory_space=pltpu.SMEM)
ANY = pl.BlockSpec(memory_space=pl.ANY)
PARAMS = pltpu.CompilerParams(vmem_limit_bytes=20 * 1024 * 1024)
SMALL = pltpu.CompilerParams(vmem_limit_bytes=20 * 1024 * 1024)


def swap(values, axis, bit):
    pairs = [(i, i ^ (1 << bit)) for i in range(lax.axis_size(axis))]
    return lax.ppermute(values, axis, pairs)


def bit_of(axis, bit):
    return (lax.axis_index(axis) >> bit) & 1


def n_bits(size):
    return size.bit_length() - 1


def pick(flag, first, second):
    return jnp.where(flag == 0, first, second)


def f32_dot(left, right, dims):
    return lax.dot_general(left, right, (dims, ((), ())), preferred_element_type=jnp.float32)


def add_rounded(mine, theirs, parts=1, axis=0):
    shape = list(mine.shape)
    shape[axis] //= parts
    return pl.pallas_call(
        functools.partial(add_kernel, axis),
        out_shape=[bf16(*shape)] * parts,
        in_specs=[VMEM, VMEM],
        out_specs=[VMEM] * parts,
        compiler_params=SMALL,
        name="add",
    )(mine, theirs)


def join(first, second):
    return pl.pallas_call(
        join_kernel,
        out_shape=bf16(2 * first.shape[0], first.shape[1]),
        in_specs=[VMEM, VMEM],
        out_specs=VMEM,
        compiler_params=SMALL,
        name="join",
    )(first, second)


def scalars(*values):
    return jnp.stack([jnp.asarray(value, jnp.int32) for value in values])


def bf16(*shape):
    return jax.ShapeDtypeStruct(shape, jnp.bfloat16)


def store_halves(flag, values, send, keep, axis):
    half = values.shape[axis] // 2
    lower, upper = (values[:half], values[half:]) if axis == 0 else (values[:, :half], values[:, half:])

    @pl.when(flag == 0)
    def _():
        keep[...] = lower
        send[...] = upper

    @pl.when(flag != 0)
    def _():
        keep[...] = upper
        send[...] = lower


def split_kernel(flags, shard, send, keep):
    store_halves(flags[0], shard[...], send, keep, 1)


def delta_kernel(flags, logit, offset, step, send, keep):
    soft_bits = jax.nn.sigmoid(logit[...])
    delta = step[...] * (soft_bits - offset[...].astype(jnp.float32))
    store_halves(flags[0], delta.astype(jnp.bfloat16), send, keep, 1)


def half_kernel(flags, shard, send, keep):
    store_halves(flags[0], shard[...], send, keep, 0)


def pair_kernel(turn, flags, own, theirs, near, far):
    own, theirs = (own[...].T, theirs[...].T) if turn else (own[...], theirs[...])
    half, cols = own.shape[0] // 2, own.shape[1]
    for flag in (0, 1):

        @pl.when(flags[0] == flag)
        def _(flag=flag):
            for lower, out in ((0, near), (half, far)):
                start = half - lower if flag else lower
                for order, (left, right) in enumerate(((own, theirs), (theirs, own))):

                    @pl.when(flags[1] == order)
                    def _(start=start, out=out, left=left, right=right):
                        out[:, :cols] = left[start : start + half]
                        out[:, cols:] = right[start : start + half]


def join_kernel(first, second, out):
    rows = first.shape[0]
    out[:rows, :] = first[...]
    out[rows:, :] = second[...]


def add_kernel(axis, mine, theirs, *outs):
    total = mine[...].astype(jnp.float32) + theirs[...].astype(jnp.float32)
    total = total.astype(jnp.bfloat16)
    size = total.shape[axis] // len(outs)
    for i, out in enumerate(outs):
        at = slice(i * size, (i + 1) * size)
        out[...] = total[at] if axis == 0 else total[:, at]


def rows_kernel(flags, near, back, own, other):
    half, cols = near.shape[0], near.shape[1] // 2
    for z, (first, second) in enumerate(((near, back), (back, near))):

        @pl.when(flags[1] == z)
        def _(first=first, second=second):
            left = jnp.concatenate([first[:, :cols], second[:, :cols]], axis=0).T
            right = jnp.concatenate([first[:, cols:], second[:, cols:]], axis=0).T

            @pl.when(flags[0] == 0)
            def _():
                own[...] = left
                other[...] = right

            @pl.when(flags[0] != 0)
            def _():
                own[...] = right
                other[...] = left


def fetch(flags, pieces, blocks, whole, held, piece_sems, block_sems):
    copies = [
        pltpu.make_async_copy(piece, whole.at[j ^ flags[0]], piece_sems.at[j])
        for j, piece in enumerate(pieces)
    ]
    moved = [
        pltpu.make_async_copy(block, held.at[k], block_sems.at[k])
        for k, block in enumerate(blocks)
    ]
    for copy in copies + moved:
        copy.start()
    return copies, moved


def times_weight(whole, held, waits):
    count, _, wide = whole.shape
    per = count // held.shape[0]
    total = None
    for i in range(count):
        if i % per == 0:
            waits[i // per].wait()
        at = (i % per) * wide
        part = f32_dot(whole[i], held[i // per, :, at : at + wide], ((1,), (1,)))
        total = part if total is None else total + part
    return total


def fisher_kernel(count, *refs):
    flags, pieces, refs = refs[0], refs[1 : count + 1], refs[count + 1 :]
    blocks, (gate, fisher, total, *scratch) = refs[:-7], refs[-7:]
    whole, held = scratch[:2]
    copies, moved = fetch(flags, pieces, blocks, *scratch)
    for copy in copies:
        copy.wait()
    grads = times_weight(whole, held, moved)
    value = ((grads * gate[...].astype(jnp.float32)) ** 2).astype(jnp.bfloat16)
    fisher[...] = value
    total[0, 0] = jnp.sum(value.astype(jnp.float32))


def residual_kernel(count, *refs):
    flags, pieces, refs = refs[0], refs[1 : count + 1], refs[count + 1 :]
    blocks, (fisher, weighted, total, *scratch) = refs[:-7], refs[-7:]
    whole, held = scratch[:2]
    copies, moved = fetch(flags, pieces, blocks, *scratch)
    for copy in copies:
        copy.wait()
    residual = times_weight(whole, held, moved)
    value = fisher[...].astype(jnp.float32) * residual
    weighted[...] = value.astype(jnp.bfloat16)
    total[0, 0] = jnp.sum(value * residual)


def grad_kernel(count, wanted, flags, *refs):
    refs, (held, sems) = refs[:-2], refs[-2:]
    grads, refs = refs[-len(wanted) :], refs[: -len(wanted)]
    half = len(refs) // 2 - 1
    blocks, weighted = refs[: 2 * half], refs[2 * half :]
    wide = grads[0].shape[1]
    per = count // half

    def copies(number, i):
        return [
            pltpu.make_async_copy(
                blocks[chunk * half + i // per], held.at[2 * number + chunk], sems.at[2 * number + chunk]
            )
            for chunk in (0, 1)
        ]

    for number, j in enumerate(wanted):
        for i in range(count):

            @pl.when(flags[0] == i ^ j)
            def _(number=number, i=i):
                for copy in copies(number, i):
                    copy.start()

    for number, j in enumerate(wanted):
        for i in range(count):

            @pl.when(flags[0] == i ^ j)
            def _(number=number, i=i):
                at = (i % per) * wide
                first, second = copies(number, i)
                first.wait()
                part = f32_dot(weighted[0][...], held[2 * number, :, at : at + wide], ((1,), (0,)))
                second.wait()
                part += f32_dot(
                    weighted[1][...], held[2 * number + 1, :, at : at + wide], ((1,), (0,))
                )
                grads[number][...] = part.astype(jnp.bfloat16)


def stack_kernel(flags, near, back, own, other):
    half, cols = near.shape[0], near.shape[1] // 2
    for z, (first, second) in enumerate(((near, back), (back, near))):

        @pl.when(flags[1] == z)
        def _(first=first, second=second):
            for at, out in enumerate((own, other)):
                out[:half, :] = first[:, at * cols : (at + 1) * cols]
                out[half:, :] = second[:, at * cols : (at + 1) * cols]


def output_kernel(count, *refs):
    flags, ups, downs = refs[0], refs[1 : count + 1], refs[count + 1 : 2 * count + 1]
    refs = refs[2 * count + 1 :]
    blocks, (gate, keep, send, *scratch) = refs[:-8], refs[-8:]
    whole, held, back, sems, block_sems = scratch
    copies, moved = fetch(flags, ups, blocks, whole, held, sems.at[0], block_sems)
    later, _ = fetch(flags, downs, (), back, held, sems.at[1], block_sems)
    for copy in copies:
        copy.wait()
    hidden = times_weight(whole, held, moved) * gate[...].astype(jnp.float32)
    hidden = hidden.astype(jnp.bfloat16)
    for copy in later:
        copy.wait()
    feats, wide = held.shape[2], whole.shape[2]
    per = count // held.shape[0]
    for i in range(count):
        k = i // per
        at = (k >> 1) * feats + (i % per) * wide
        out = send if k & 1 else keep
        part = f32_dot(hidden, back[i], ((0,), (0,)))
        out[:, at : at + wide] = part.astype(jnp.bfloat16)


class Plan:
    def __init__(self):
        self.steps, self.got, self.flying, self.token = {}, {}, {}, None

    def tie(self, values):
        values, self.token = lax.optimization_barrier((values, self.token))
        return values

    def exchange(self, name, axis, bit, source):
        def start():
            self.flying[name] = swap(self.tie(source()), axis, bit)

        def wait():
            self.got[name] = self.tie(self.flying.pop(name))

        self.steps["s " + name], self.steps["w " + name] = start, wait

    def compute(self, name, function, tied=True):
        def run():
            values = function()
            self.got[name] = self.tie(values) if tied else values

        self.steps["c " + name] = run

    def run(self, token, order):
        self.token = token
        steps = list(self.steps.values())
        if len(order) != len(steps):
            order = range(len(steps))
        for number in order:
            steps[number]()
        return self.got


def plan_pair(plan, name, first, order, turn):
    got = plan.got
    plan.compute("p" + name, first)
    plan.exchange(name + "_y", "dp", 0, lambda: got["p" + name][0])

    def pair():
        own, theirs = got["p" + name][1], got[name + "_y"]
        rows, cols = own.shape[::-1] if turn else own.shape
        out = bf16(rows // 2, 2 * cols)
        return pl.pallas_call(
            functools.partial(pair_kernel, turn),
            out_shape=(out, out),
            in_specs=[SMEM, VMEM, VMEM],
            out_specs=(VMEM, VMEM),
            compiler_params=SMALL,
            name="pair",
        )(scalars(bit_of("dp", 1), order), own, theirs)

    plan.compute("k" + name, pair)
    plan.exchange(name + "_zl", "dp", 1, lambda: got["k" + name][1])


def plan_weight(plan, name, first, nb):
    got = plan.got
    plan_pair(plan, name, first, bit_of("dp", 0), True)
    pieces = [lambda: got["k" + name][0], lambda: got[name + "_zl"]]
    for bit in range(2, nb):
        for piece in list(pieces):
            key = name + "_h" + str(len(pieces) - 2)
            plan.exchange(key, "dp", bit, piece)
            pieces.append(lambda key=key: got[key])
    return lambda: [piece() for piece in pieces]


def plan_tokens(plan, name, shard, nt):
    got, chunks = plan.got, {}
    plan.exchange(name + "b_zl", "dp", 1, lambda: shard)
    for chunk, own in (("a", lambda: shard), ("b", lambda: got[name + "b_zl"])):
        key = name + chunk
        plan.exchange(key + "_y", "dp", 0, own)
        plan.compute(
            "c" + key,
            lambda own=own, key=key: join(own(), got[key + "_y"]),
        )
        blocks = ["c" + key]
        for bit in range(nt - 1, -1, -1):
            new = []
            for index, block in enumerate(blocks):
                part = key + "_t" + str(bit) + str(index)
                plan.exchange(part, "tensor", bit, lambda block=block: got[block])
                new += [block, part]
            blocks = new
        chunks[chunk] = blocks
    return lambda chunk: [got[key] for key in chunks[chunk]]


def plan_collect(plan, name, near, away):
    got = plan.got
    y, z = bit_of("dp", 0), bit_of("dp", 1)
    plan.exchange(name + "_zl", "dp", 1, away)

    def stack():
        out = bf16(2 * near().shape[0], near().shape[1] // 2)
        return pl.pallas_call(
            stack_kernel,
            out_shape=(out, out),
            in_specs=[SMEM, VMEM, VMEM],
            out_specs=(VMEM, VMEM),
            compiler_params=SMALL,
            name="stack",
        )(scalars(y, z), near(), got[name + "_zl"])

    plan.compute("p" + name, stack)
    plan.exchange(name + "_y", "dp", 0, lambda: got["p" + name][1])

    def whole():
        own, theirs = got["p" + name][0], got[name + "_y"]
        return jnp.concatenate([pick(y, own, theirs), pick(y, theirs, own)], axis=0)

    return whole


def plan_scatter(plan, full, nb):
    got = plan.got
    y, z = bit_of("dp", 0), bit_of("dp", 1)
    half, number, pieces = 1 << (nb - 2), 0, []
    for index in range(2 * half):
        pieces.append(lambda index=index: full(index))
    for bit in range(nb - 1, 1, -1):
        half = len(pieces) // 2
        sums = []
        for index in reversed(range(half)):
            name = "R_h" + str(number)
            plan.exchange(name, "dp", bit, pieces[half + index])
            plan.compute(
                "a" + str(number),
                lambda mine=pieces[index], name=name: add_rounded(mine(), got[name])[0],
            )
            sums.insert(0, lambda key="a" + str(number): got[key])
            number += 1
        pieces = sums
    near, away = pieces
    plan.exchange("R_zl", "dp", 1, away)

    def rows():
        out = bf16(near().shape[1] // 2, 2 * near().shape[0])
        return pl.pallas_call(
            rows_kernel,
            out_shape=(out, out),
            in_specs=[SMEM, VMEM, VMEM],
            out_specs=(VMEM, VMEM),
            compiler_params=SMALL,
            name="rows",
        )(scalars(y, z), near(), got["R_zl"])

    plan.compute("ry", rows)
    plan.exchange("R_y", "dp", 0, lambda: got["ry"][1])

    def whole():
        own, theirs = got["ry"][0], got["R_y"]
        return jnp.concatenate([pick(y, own, theirs), pick(y, theirs, own)], axis=1)

    return whole


def plan_output(plan, part, tok, nt):
    got = plan.got
    for chunk in "ba":
        key = "O" + chunk
        plan.compute("kC" + chunk, lambda chunk=chunk: part(chunk))
        plan.exchange(key + "_t0", "tensor", 0, lambda chunk=chunk: got["kC" + chunk][1])
        last = "o0" + chunk
        plan.compute(
            last,
            lambda chunk=chunk, key=key: add_rounded(
                got["kC" + chunk][0], got[key + "_t0"], 2, int(nt > 1)
            ),
        )
        for bit in range(nt - 1, 0, -1):
            name, step = key + "_t" + str(bit), "o" + str(bit) + chunk
            plan.exchange(name, "tensor", bit, lambda last=last: got[last][1])
            plan.compute(
                step,
                lambda last=last, name=name, bit=bit: add_rounded(
                    got[last][0], got[name], 2, int(bit > 1)
                ),
            )
            last = step
        plan.exchange(key + "_y", "dp", 0, lambda last=last: got[last][1])
        plan.compute(
            "oy" + chunk,
            lambda last=last, key=key: add_rounded(got[last][0], got[key + "_y"])[0],
        )
        if chunk == "b":
            plan.exchange("O_zl", "dp", 1, lambda: got["oyb"])
    return lambda: add_rounded(got["oya"], got["O_zl"])[0]


def body(
    block_input, gate_act, grad_out, up_weight, down_weight, quant_step, round_logit, grid_offset
):
    n_dp, n_tensor = lax.axis_size("dp"), lax.axis_size("tensor")
    nb, nt = n_bits(n_dp), n_bits(n_tensor)
    tok, cols = gate_act.shape
    half, quarter = cols // 2, cols // 4
    rows = up_weight.shape[0]
    feats = block_input.shape[1]
    depth = rows * n_dp
    count = n_dp // 2
    y = bit_of("dp", 0)
    shift = (lax.axis_index("dp") >> 1) ^ (lax.axis_index("tensor") << (nb - 1 - nt))

    soft_bits = jax.nn.sigmoid(round_logit)
    centered = 2.0 * soft_bits - 1.0
    reg_local = jnp.sum(1.0 - (centered * centered) ** 2)

    def split(name, kernel, out, *operands):
        return pl.pallas_call(
            kernel,
            out_shape=(out, out),
            in_specs=[SMEM] + [VMEM] * len(operands),
            out_specs=(VMEM, VMEM),
            compiler_params=SMALL,
            name=name,
        )(scalars(y), *operands)

    plan = Plan()
    got = plan.got
    out = bf16(rows, half)
    down = plan_weight(plan, "D", lambda: split("split", split_kernel, out, down_weight.T), nb)
    grads = plan_tokens(plan, "G", grad_out, nt)
    plan_pair(
        plan, "g", lambda: split("split", half_kernel, bf16(half, tok), gate_act.T), 0, False
    )
    gate = lambda chunk: got["kg"][0] if chunk == "a" else got["g_zl"]
    delta = plan_weight(
        plan,
        "T",
        lambda: split(
            "delta", delta_kernel, out, round_logit, grid_offset, quant_step[None, :]
        ),
        nb,
    )
    features = plan_tokens(plan, "X", block_input, nt)
    up = plan_weight(plan, "U", lambda: split("split", split_kernel, out, up_weight), nb)
    whole = pltpu.VMEM((count, quarter, 2 * rows), jnp.bfloat16)
    held = pltpu.VMEM((n_tensor, 2 * tok, feats), jnp.bfloat16)
    sems = pltpu.SemaphoreType.DMA

    def matmuls(name, kernel, out_shape, out_specs, scratch, *operands):
        return pl.pallas_call(
            functools.partial(kernel, count),
            out_shape=out_shape,
            in_specs=[SMEM] + [ANY] * (len(operands) - 1) + [VMEM],
            out_specs=out_specs,
            scratch_shapes=scratch,
            compiler_params=PARAMS,
            name=name,
        )(scalars(shift), *operands)

    simple = [whole, held, sems((count,)), sems((n_tensor,))]
    one = jax.ShapeDtypeStruct((1, 1), jnp.float32)
    for chunk in "ab":
        plan.compute(
            "kA" + chunk,
            lambda chunk=chunk: matmuls(
                "fisher_matmul",
                fisher_kernel,
                (bf16(quarter, 2 * tok), one),
                (VMEM, SMEM),
                simple,
                *down(),
                *grads(chunk),
                gate(chunk),
            ),
        )
    fisher = lambda chunk: got["kA" + chunk][0]
    for chunk in "ab":
        plan.compute(
            "kR" + chunk,
            lambda chunk=chunk: matmuls(
                "residual_matmul",
                residual_kernel,
                (bf16(quarter, 2 * tok), one),
                (VMEM, SMEM),
                simple,
                *delta(),
                *features(chunk),
                fisher(chunk),
            ),
        )

    def make_grad(wanted):
        operands = *features("a"), *features("b"), got["kRa"][0], got["kRb"][0]
        return pl.pallas_call(
            functools.partial(grad_kernel, count, wanted),
            out_shape=[bf16(quarter, 2 * rows)] * len(wanted),
            in_specs=[SMEM] + [ANY] * (len(operands) - 2) + [VMEM, VMEM],
            out_specs=[VMEM] * len(wanted),
            scratch_shapes=[
                pltpu.VMEM((2 * len(wanted), 2 * tok, feats), jnp.bfloat16),
                sems((2 * len(wanted),)),
            ],
            compiler_params=PARAMS,
            name="grad_matmul",
        )(scalars(shift), *operands)

    parts = [(j,) for j in reversed(range(count // 2, count))] + [tuple(range(count // 2))]
    where = {}
    for number, wanted in enumerate(parts):
        plan.compute("r" + str(number), lambda wanted=wanted: make_grad(wanted))
        for at, j in enumerate(wanted):
            where[j] = "r" + str(number), at
    grad_rows = plan_scatter(plan, lambda j: got[where[j][0]][where[j][1]], nb)
    fisher_rows = plan_collect(plan, "f", lambda: fisher("a"), lambda: fisher("b"))
    pair = bf16(2 * tok, depth // 2)
    out_rows = plan_output(
        plan,
        lambda chunk: matmuls(
            "output_matmul",
            output_kernel,
            (pair, pair),
            (VMEM, VMEM),
            [whole, held, whole, sems((2, count)), sems((n_tensor,))],
            *up(),
            *down(),
            *features(chunk),
            gate(chunk),
        ),
        tok,
        nt,
    )

    last = lambda: jnp.concatenate(
        [got["kAa"][1] + got["kAb"][1], got["kRa"][1] + got["kRb"][1], reg_local[None, None]], axis=1
    )
    for axis, bits in (("dp", nb), ("tensor", nt)):
        for bit in range(bits):
            name = "s_" + axis + str(bit)
            plan.exchange(name, axis, bit, last)
            plan.compute("q" + name, lambda last=last, name=name: last() + got[name], tied=False)
            last = lambda name=name: got["q" + name]

    plan.run(lax.axis_index("dp"), ORDER)

    sums = last()[0]
    fisher_sum, recon_total, reg_total = sums[0], sums[1], sums[2]
    total_cells = n_dp * n_tensor * tok * cols
    weight_cells = depth * n_tensor * cols
    fisher_mean = fisher_sum / total_cells
    sig_slope = soft_bits * (1.0 - soft_bits)
    grad_logit = (
        grad_rows().astype(jnp.float32)
        * (2.0 / fisher_mean)
        * quant_step[None, :]
        * sig_slope
        - reg_weight * 8.0 * centered**3 * sig_slope
    )
    loss = recon_total / (fisher_mean * total_cells) + reg_weight * reg_total / weight_cells
    loss = jnp.where(plan.token < 0, -loss, loss)
    return (out_rows(), fisher_rows().T, grad_logit, loss)


def solution(mesh):
    placed = (
        P("dp", "tensor"),
        P("dp", "tensor"),
        P("dp", "tensor"),
        P("dp", "tensor"),
        P("tensor", "dp"),
        P("tensor"),
        P("dp", "tensor"),
        P("dp", "tensor"),
    )
    return jax.shard_map(
        body,
        mesh=mesh,
        in_specs=placed,
        out_specs=(P("dp", "tensor"), P("dp", "tensor"), P("dp", "tensor"), P()),
        check_vma=False,
    )
```

```python
import functools

import jax
import jax.numpy as jnp
from jax import lax
from jax.experimental import pallas as pl
from jax.experimental.pallas import tpu as pltpu
from jax.sharding import PartitionSpec as P

reg_weight = 0.5

ORDER = (
    46,
    48,
    66,
    67,
    0,
    1,
    30,
    10,
    36,
    37,
    49,
    50,
    51,
    47,
    68,
    69,
    72,
    70,
    11,
    21,
    57,
    2,
    3,
    58,
    71,
    74,
    52,
    4,
    31,
    55,
    59,
    60,
    73,
    6,
    22,
    23,
    26,
    24,
    38,
    39,
    42,
    40,
    5,
    75,
    12,
    32,
    33,
    61,
    64,
    53,
    13,
    7,
    62,
    14,
    15,
    41,
    44,
    25,
    8,
    65,
    34,
    16,
    17,
    19,
    63,
    9,
    54,
    35,
    99,
    100,
    56,
    27,
    20,
    111,
    18,
    45,
    112,
    28,
    76,
    101,
    102,
    103,
    113,
    114,
    29,
    77,
    94,
    43,
    78,
    79,
    121,
    80,
    83,
    115,
    82,
    95,
    104,
    105,
    106,
    96,
    97,
    81,
    86,
    122,
    123,
    84,
    124,
    85,
    89,
    107,
    116,
    117,
    118,
    108,
    125,
    126,
    98,
    109,
    127,
    87,
    88,
    119,
    128,
    90,
    91,
    92,
    120,
    129,
    130,
    131,
    132,
    110,
    133,
    134,
    135,
    93,
)

VMEM = pl.BlockSpec(memory_space=pltpu.VMEM)
SMEM = pl.BlockSpec(memory_space=pltpu.SMEM)
ANY = pl.BlockSpec(memory_space=pl.ANY)
PARAMS = pltpu.CompilerParams(vmem_limit_bytes=20 * 1024 * 1024)
SMALL = pltpu.CompilerParams(vmem_limit_bytes=20 * 1024 * 1024)


def swap(values, axis, bit):
    pairs = [(i, i ^ (1 << bit)) for i in range(lax.axis_size(axis))]
    return lax.ppermute(values, axis, pairs)


def bit_of(axis, bit):
    return (lax.axis_index(axis) >> bit) & 1


def n_bits(size):
    return size.bit_length() - 1


def pick(flag, first, second):
    return jnp.where(flag == 0, first, second)


def f32_dot(left, right, dims):
    return lax.dot_general(left, right, (dims, ((), ())), preferred_element_type=jnp.float32)


def add_rounded(mine, theirs, parts=1, axis=0):
    shape = list(mine.shape)
    shape[axis] //= parts
    return pl.pallas_call(
        functools.partial(add_kernel, axis),
        out_shape=[bf16(*shape)] * parts,
        in_specs=[VMEM, VMEM],
        out_specs=[VMEM] * parts,
        compiler_params=SMALL,
        name="add",
    )(mine, theirs)


def join(first, second):
    return pl.pallas_call(
        join_kernel,
        out_shape=bf16(2 * first.shape[0], first.shape[1]),
        in_specs=[VMEM, VMEM],
        out_specs=VMEM,
        compiler_params=SMALL,
        name="join",
    )(first, second)


def scalars(*values):
    return jnp.stack([jnp.asarray(value, jnp.int32) for value in values])


def bf16(*shape):
    return jax.ShapeDtypeStruct(shape, jnp.bfloat16)


def store_halves(flag, values, send, keep, axis):
    half = values.shape[axis] // 2
    lower, upper = (values[:half], values[half:]) if axis == 0 else (values[:, :half], values[:, half:])

    @pl.when(flag == 0)
    def _():
        keep[...] = lower
        send[...] = upper

    @pl.when(flag != 0)
    def _():
        keep[...] = upper
        send[...] = lower


def split_kernel(flags, shard, send, keep):
    store_halves(flags[0], shard[...], send, keep, 1)


def delta_kernel(flags, logit, offset, step, send, keep):
    soft_bits = jax.nn.sigmoid(logit[...])
    delta = step[...] * (soft_bits - offset[...].astype(jnp.float32))
    store_halves(flags[0], delta.astype(jnp.bfloat16), send, keep, 1)


def half_kernel(flags, shard, send, keep):
    store_halves(flags[0], shard[...], send, keep, 0)


def pair_kernel(turn, flags, own, theirs, near, far):
    own, theirs = (own[...].T, theirs[...].T) if turn else (own[...], theirs[...])
    half, cols = own.shape[0] // 2, own.shape[1]
    for flag in (0, 1):

        @pl.when(flags[0] == flag)
        def _(flag=flag):
            for lower, out in ((0, near), (half, far)):
                start = half - lower if flag else lower
                for order, (left, right) in enumerate(((own, theirs), (theirs, own))):

                    @pl.when(flags[1] == order)
                    def _(start=start, out=out, left=left, right=right):
                        out[:, :cols] = left[start : start + half]
                        out[:, cols:] = right[start : start + half]


def join_kernel(first, second, out):
    rows = first.shape[0]
    out[:rows, :] = first[...]
    out[rows:, :] = second[...]


def add_kernel(axis, mine, theirs, *outs):
    total = mine[...].astype(jnp.float32) + theirs[...].astype(jnp.float32)
    total = total.astype(jnp.bfloat16)
    size = total.shape[axis] // len(outs)
    for i, out in enumerate(outs):
        at = slice(i * size, (i + 1) * size)
        out[...] = total[at] if axis == 0 else total[:, at]


def rows_kernel(flags, near, back, own, other):
    half, cols = near.shape[0], near.shape[1] // 2
    for z, (first, second) in enumerate(((near, back), (back, near))):

        @pl.when(flags[1] == z)
        def _(first=first, second=second):
            left = jnp.concatenate([first[:, :cols], second[:, :cols]], axis=0).T
            right = jnp.concatenate([first[:, cols:], second[:, cols:]], axis=0).T

            @pl.when(flags[0] == 0)
            def _():
                own[...] = left
                other[...] = right

            @pl.when(flags[0] != 0)
            def _():
                own[...] = right
                other[...] = left


def fetch(flags, pieces, blocks, whole, held, piece_sems, block_sems):
    copies = [
        pltpu.make_async_copy(piece, whole.at[j ^ flags[0]], piece_sems.at[j])
        for j, piece in enumerate(pieces)
    ]
    moved = [
        pltpu.make_async_copy(block, held.at[k], block_sems.at[k])
        for k, block in enumerate(blocks)
    ]
    for copy in copies + moved:
        copy.start()
    return copies, moved


def times_weight(whole, held, waits):
    count, _, wide = whole.shape
    per = count // held.shape[0]
    total = None
    for i in range(count):
        if i % per == 0:
            waits[i // per].wait()
        at = (i % per) * wide
        part = f32_dot(whole[i], held[i // per, :, at : at + wide], ((1,), (1,)))
        total = part if total is None else total + part
    return total


def fisher_kernel(count, *refs):
    flags, pieces, refs = refs[0], refs[1 : count + 1], refs[count + 1 :]
    blocks, (gate, fisher, total, *scratch) = refs[:-7], refs[-7:]
    whole, held = scratch[:2]
    copies, moved = fetch(flags, pieces, blocks, *scratch)
    for copy in copies:
        copy.wait()
    grads = times_weight(whole, held, moved)
    value = ((grads * gate[...].astype(jnp.float32)) ** 2).astype(jnp.bfloat16)
    fisher[...] = value
    total[0, 0] = jnp.sum(value.astype(jnp.float32))


def residual_kernel(count, *refs):
    flags, pieces, refs = refs[0], refs[1 : count + 1], refs[count + 1 :]
    blocks, (fisher, weighted, total, *scratch) = refs[:-7], refs[-7:]
    whole, held = scratch[:2]
    copies, moved = fetch(flags, pieces, blocks, *scratch)
    for copy in copies:
        copy.wait()
    residual = times_weight(whole, held, moved)
    value = fisher[...].astype(jnp.float32) * residual
    weighted[...] = value.astype(jnp.bfloat16)
    total[0, 0] = jnp.sum(value * residual)


def grad_kernel(count, wanted, flags, *refs):
    refs, (held, sems) = refs[:-2], refs[-2:]
    grads, refs = refs[-len(wanted) :], refs[: -len(wanted)]
    half = len(refs) // 2 - 1
    blocks, weighted = refs[: 2 * half], refs[2 * half :]
    wide = grads[0].shape[1]
    per = count // half

    def copies(number, i):
        return [
            pltpu.make_async_copy(
                blocks[chunk * half + i // per], held.at[2 * number + chunk], sems.at[2 * number + chunk]
            )
            for chunk in (0, 1)
        ]

    for number, j in enumerate(wanted):
        for i in range(count):

            @pl.when(flags[0] == i ^ j)
            def _(number=number, i=i):
                for copy in copies(number, i):
                    copy.start()

    for number, j in enumerate(wanted):
        for i in range(count):

            @pl.when(flags[0] == i ^ j)
            def _(number=number, i=i):
                at = (i % per) * wide
                first, second = copies(number, i)
                first.wait()
                part = f32_dot(weighted[0][...], held[2 * number, :, at : at + wide], ((1,), (0,)))
                second.wait()
                part += f32_dot(
                    weighted[1][...], held[2 * number + 1, :, at : at + wide], ((1,), (0,))
                )
                grads[number][...] = part.astype(jnp.bfloat16)


def stack_kernel(flags, near, back, own, other):
    half, cols = near.shape[0], near.shape[1] // 2
    for z, (first, second) in enumerate(((near, back), (back, near))):

        @pl.when(flags[1] == z)
        def _(first=first, second=second):
            for at, out in enumerate((own, other)):
                out[:half, :] = first[:, at * cols : (at + 1) * cols]
                out[half:, :] = second[:, at * cols : (at + 1) * cols]


def output_kernel(count, *refs):
    flags, ups, downs = refs[0], refs[1 : count + 1], refs[count + 1 : 2 * count + 1]
    refs = refs[2 * count + 1 :]
    blocks, (gate, keep, send, *scratch) = refs[:-8], refs[-8:]
    whole, held, back, sems, block_sems = scratch
    copies, moved = fetch(flags, ups, blocks, whole, held, sems.at[0], block_sems)
    later, _ = fetch(flags, downs, (), back, held, sems.at[1], block_sems)
    for copy in copies:
        copy.wait()
    hidden = times_weight(whole, held, moved) * gate[...].astype(jnp.float32)
    hidden = hidden.astype(jnp.bfloat16)
    for copy in later:
        copy.wait()
    feats, wide = held.shape[2], whole.shape[2]
    per = count // held.shape[0]
    for i in range(count):
        k = i // per
        at = (k >> 1) * feats + (i % per) * wide
        out = send if k & 1 else keep
        part = f32_dot(hidden, back[i], ((0,), (0,)))
        out[:, at : at + wide] = part.astype(jnp.bfloat16)


class Plan:
    def __init__(self):
        self.steps, self.got, self.flying, self.token = {}, {}, {}, None

    def tie(self, values):
        values, self.token = lax.optimization_barrier((values, self.token))
        return values

    def exchange(self, name, axis, bit, source):
        def start():
            self.flying[name] = swap(self.tie(source()), axis, bit)

        def wait():
            self.got[name] = self.tie(self.flying.pop(name))

        self.steps["s " + name], self.steps["w " + name] = start, wait

    def compute(self, name, function, tied=True):
        def run():
            values = function()
            self.got[name] = self.tie(values) if tied else values

        self.steps["c " + name] = run

    def run(self, token, order):
        self.token = token
        steps = list(self.steps.values())
        if len(order) != len(steps):
            order = range(len(steps))
        for number in order:
            steps[number]()
        return self.got


def plan_pair(plan, name, first, order, turn):
    got = plan.got
    plan.compute("p" + name, first)
    plan.exchange(name + "_y", "dp", 0, lambda: got["p" + name][0])

    def pair():
        own, theirs = got["p" + name][1], got[name + "_y"]
        rows, cols = own.shape[::-1] if turn else own.shape
        out = bf16(rows // 2, 2 * cols)
        return pl.pallas_call(
            functools.partial(pair_kernel, turn),
            out_shape=(out, out),
            in_specs=[SMEM, VMEM, VMEM],
            out_specs=(VMEM, VMEM),
            compiler_params=SMALL,
            name="pair",
        )(scalars(bit_of("dp", 1), order), own, theirs)

    plan.compute("k" + name, pair)
    plan.exchange(name + "_zl", "dp", 1, lambda: got["k" + name][1])


def plan_weight(plan, name, first, nb):
    got = plan.got
    plan_pair(plan, name, first, bit_of("dp", 0), True)
    pieces = [lambda: got["k" + name][0], lambda: got[name + "_zl"]]
    for bit in range(2, nb):
        for piece in list(pieces):
            key = name + "_h" + str(len(pieces) - 2)
            plan.exchange(key, "dp", bit, piece)
            pieces.append(lambda key=key: got[key])
    return lambda: [piece() for piece in pieces]


def plan_tokens(plan, name, shard, nt):
    got, chunks = plan.got, {}
    plan.exchange(name + "b_zl", "dp", 1, lambda: shard)
    for chunk, own in (("a", lambda: shard), ("b", lambda: got[name + "b_zl"])):
        key = name + chunk
        plan.exchange(key + "_y", "dp", 0, own)
        plan.compute(
            "c" + key,
            lambda own=own, key=key: join(own(), got[key + "_y"]),
        )
        blocks = ["c" + key]
        for bit in range(nt - 1, -1, -1):
            new = []
            for index, block in enumerate(blocks):
                part = key + "_t" + str(bit) + str(index)
                plan.exchange(part, "tensor", bit, lambda block=block: got[block])
                new += [block, part]
            blocks = new
        chunks[chunk] = blocks
    return lambda chunk: [got[key] for key in chunks[chunk]]


def plan_collect(plan, name, near, away):
    got = plan.got
    y, z = bit_of("dp", 0), bit_of("dp", 1)
    plan.exchange(name + "_zl", "dp", 1, away)

    def stack():
        out = bf16(2 * near().shape[0], near().shape[1] // 2)
        return pl.pallas_call(
            stack_kernel,
            out_shape=(out, out),
            in_specs=[SMEM, VMEM, VMEM],
            out_specs=(VMEM, VMEM),
            compiler_params=SMALL,
            name="stack",
        )(scalars(y, z), near(), got[name + "_zl"])

    plan.compute("p" + name, stack)
    plan.exchange(name + "_y", "dp", 0, lambda: got["p" + name][1])

    def whole():
        own, theirs = got["p" + name][0], got[name + "_y"]
        return jnp.concatenate([pick(y, own, theirs), pick(y, theirs, own)], axis=0)

    return whole


def plan_scatter(plan, full, nb):
    got = plan.got
    y, z = bit_of("dp", 0), bit_of("dp", 1)
    half, number, pieces = 1 << (nb - 2), 0, []
    for index in range(2 * half):
        pieces.append(lambda index=index: full(index))
    for bit in range(nb - 1, 1, -1):
        half = len(pieces) // 2
        sums = []
        for index in reversed(range(half)):
            name = "R_h" + str(number)
            plan.exchange(name, "dp", bit, pieces[half + index])
            plan.compute(
                "a" + str(number),
                lambda mine=pieces[index], name=name: add_rounded(mine(), got[name])[0],
            )
            sums.insert(0, lambda key="a" + str(number): got[key])
            number += 1
        pieces = sums
    near, away = pieces
    plan.exchange("R_zl", "dp", 1, away)

    def rows():
        out = bf16(near().shape[1] // 2, 2 * near().shape[0])
        return pl.pallas_call(
            rows_kernel,
            out_shape=(out, out),
            in_specs=[SMEM, VMEM, VMEM],
            out_specs=(VMEM, VMEM),
            compiler_params=SMALL,
            name="rows",
        )(scalars(y, z), near(), got["R_zl"])

    plan.compute("ry", rows)
    plan.exchange("R_y", "dp", 0, lambda: got["ry"][1])

    def whole():
        own, theirs = got["ry"][0], got["R_y"]
        return jnp.concatenate([pick(y, own, theirs), pick(y, theirs, own)], axis=1)

    return whole


def plan_output(plan, part, tok, nt):
    got = plan.got
    for chunk in "ba":
        key = "O" + chunk
        plan.compute("kC" + chunk, lambda chunk=chunk: part(chunk))
        plan.exchange(key + "_t0", "tensor", 0, lambda chunk=chunk: got["kC" + chunk][1])
        last = "o0" + chunk
        plan.compute(
            last,
            lambda chunk=chunk, key=key: add_rounded(
                got["kC" + chunk][0], got[key + "_t0"], 2, int(nt > 1)
            ),
        )
        for bit in range(nt - 1, 0, -1):
            name, step = key + "_t" + str(bit), "o" + str(bit) + chunk
            plan.exchange(name, "tensor", bit, lambda last=last: got[last][1])
            plan.compute(
                step,
                lambda last=last, name=name, bit=bit: add_rounded(
                    got[last][0], got[name], 2, int(bit > 1)
                ),
            )
            last = step
        plan.exchange(key + "_y", "dp", 0, lambda last=last: got[last][1])
        plan.compute(
            "oy" + chunk,
            lambda last=last, key=key: add_rounded(got[last][0], got[key + "_y"])[0],
        )
        if chunk == "b":
            plan.exchange("O_zl", "dp", 1, lambda: got["oyb"])
    return lambda: add_rounded(got["oya"], got["O_zl"])[0]


def body(
    block_input, gate_act, grad_out, up_weight, down_weight, quant_step, round_logit, grid_offset
):
    n_dp, n_tensor = lax.axis_size("dp"), lax.axis_size("tensor")
    nb, nt = n_bits(n_dp), n_bits(n_tensor)
    tok, cols = gate_act.shape
    half, quarter = cols // 2, cols // 4
    rows = up_weight.shape[0]
    feats = block_input.shape[1]
    depth = rows * n_dp
    count = n_dp // 2
    y = bit_of("dp", 0)
    shift = (lax.axis_index("dp") >> 1) ^ (lax.axis_index("tensor") << (nb - 1 - nt))

    soft_bits = jax.nn.sigmoid(round_logit)
    centered = 2.0 * soft_bits - 1.0
    reg_local = jnp.sum(1.0 - (centered * centered) ** 2)

    def split(name, kernel, out, *operands):
        return pl.pallas_call(
            kernel,
            out_shape=(out, out),
            in_specs=[SMEM] + [VMEM] * len(operands),
            out_specs=(VMEM, VMEM),
            compiler_params=SMALL,
            name=name,
        )(scalars(y), *operands)

    plan = Plan()
    got = plan.got
    out = bf16(rows, half)
    down = plan_weight(plan, "D", lambda: split("split", split_kernel, out, down_weight.T), nb)
    grads = plan_tokens(plan, "G", grad_out, nt)
    plan_pair(
        plan, "g", lambda: split("split", half_kernel, bf16(half, tok), gate_act.T), 0, False
    )
    gate = lambda chunk: got["kg"][0] if chunk == "a" else got["g_zl"]
    delta = plan_weight(
        plan,
        "T",
        lambda: split(
            "delta", delta_kernel, out, round_logit, grid_offset, quant_step[None, :]
        ),
        nb,
    )
    features = plan_tokens(plan, "X", block_input, nt)
    up = plan_weight(plan, "U", lambda: split("split", split_kernel, out, up_weight), nb)
    whole = pltpu.VMEM((count, quarter, 2 * rows), jnp.bfloat16)
    held = pltpu.VMEM((n_tensor, 2 * tok, feats), jnp.bfloat16)
    sems = pltpu.SemaphoreType.DMA

    def matmuls(name, kernel, out_shape, out_specs, scratch, *operands):
        return pl.pallas_call(
            functools.partial(kernel, count),
            out_shape=out_shape,
            in_specs=[SMEM] + [ANY] * (len(operands) - 1) + [VMEM],
            out_specs=out_specs,
            scratch_shapes=scratch,
            compiler_params=PARAMS,
            name=name,
        )(scalars(shift), *operands)

    simple = [whole, held, sems((count,)), sems((n_tensor,))]
    one = jax.ShapeDtypeStruct((1, 1), jnp.float32)
    for chunk in "ab":
        plan.compute(
            "kA" + chunk,
            lambda chunk=chunk: matmuls(
                "fisher_matmul",
                fisher_kernel,
                (bf16(quarter, 2 * tok), one),
                (VMEM, SMEM),
                simple,
                *down(),
                *grads(chunk),
                gate(chunk),
            ),
        )
    fisher = lambda chunk: got["kA" + chunk][0]
    for chunk in "ab":
        plan.compute(
            "kR" + chunk,
            lambda chunk=chunk: matmuls(
                "residual_matmul",
                residual_kernel,
                (bf16(quarter, 2 * tok), one),
                (VMEM, SMEM),
                simple,
                *delta(),
                *features(chunk),
                fisher(chunk),
            ),
        )

    def make_grad(wanted):
        operands = *features("a"), *features("b"), got["kRa"][0], got["kRb"][0]
        return pl.pallas_call(
            functools.partial(grad_kernel, count, wanted),
            out_shape=[bf16(quarter, 2 * rows)] * len(wanted),
            in_specs=[SMEM] + [ANY] * (len(operands) - 2) + [VMEM, VMEM],
            out_specs=[VMEM] * len(wanted),
            scratch_shapes=[
                pltpu.VMEM((2 * len(wanted), 2 * tok, feats), jnp.bfloat16),
                sems((2 * len(wanted),)),
            ],
            compiler_params=PARAMS,
            name="grad_matmul",
        )(scalars(shift), *operands)

    parts = [(j,) for j in reversed(range(count // 2, count))] + [tuple(range(count // 2))]
    where = {}
    for number, wanted in enumerate(parts):
        plan.compute("r" + str(number), lambda wanted=wanted: make_grad(wanted))
        for at, j in enumerate(wanted):
            where[j] = "r" + str(number), at
    grad_rows = plan_scatter(plan, lambda j: got[where[j][0]][where[j][1]], nb)
    fisher_rows = plan_collect(plan, "f", lambda: fisher("a"), lambda: fisher("b"))
    pair = bf16(2 * tok, depth // 2)
    out_rows = plan_output(
        plan,
        lambda chunk: matmuls(
            "output_matmul",
            output_kernel,
            (pair, pair),
            (VMEM, VMEM),
            [whole, held, whole, sems((2, count)), sems((n_tensor,))],
            *up(),
            *down(),
            *features(chunk),
            gate(chunk),
        ),
        tok,
        nt,
    )

    last = lambda: jnp.concatenate(
        [got["kAa"][1] + got["kAb"][1], got["kRa"][1] + got["kRb"][1], reg_local[None, None]], axis=1
    )
    for axis, bits in (("dp", nb), ("tensor", nt)):
        for bit in range(bits):
            name = "s_" + axis + str(bit)
            plan.exchange(name, axis, bit, last)
            plan.compute("q" + name, lambda last=last, name=name: last() + got[name], tied=False)
            last = lambda name=name: got["q" + name]

    plan.run(lax.axis_index("dp"), ORDER)

    sums = last()[0]
    fisher_sum, recon_total, reg_total = sums[0], sums[1], sums[2]
    total_cells = n_dp * n_tensor * tok * cols
    weight_cells = depth * n_tensor * cols
    fisher_mean = fisher_sum / total_cells
    sig_slope = soft_bits * (1.0 - soft_bits)
    grad_logit = (
        grad_rows().astype(jnp.float32)
        * (2.0 / fisher_mean)
        * quant_step[None, :]
        * sig_slope
        - reg_weight * 8.0 * centered**3 * sig_slope
    )
    loss = recon_total / (fisher_mean * total_cells) + reg_weight * reg_total / weight_cells
    loss = jnp.where(plan.token < 0, -loss, loss)
    return (out_rows(), fisher_rows().T, grad_logit, loss)


def solution(mesh):
    placed = (
        P("dp", "tensor"),
        P("dp", "tensor"),
        P("dp", "tensor"),
        P("dp", "tensor"),
        P("tensor", "dp"),
        P("tensor"),
        P("dp", "tensor"),
        P("dp", "tensor"),
    )
    return jax.shard_map(
        body,
        mesh=mesh,
        in_specs=placed,
        out_specs=(P("dp", "tensor"), P("dp", "tensor"), P("dp", "tensor"), P()),
        check_vma=False,
    )
```

```python
import functools

import jax
import jax.numpy as jnp
from jax import lax
from jax.experimental import pallas as pl
from jax.experimental.pallas import tpu as pltpu
from jax.sharding import PartitionSpec as P

reg_weight = 0.5

ORDER = (
    46,
    0,
    12,
    1,
    66,
    36,
    30,
    67,
    47,
    10,
    2,
    3,
    57,
    37,
    6,
    11,
    4,
    68,
    69,
    21,
    38,
    39,
    40,
    7,
    72,
    48,
    70,
    5,
    22,
    23,
    8,
    24,
    13,
    73,
    58,
    41,
    31,
    14,
    59,
    25,
    26,
    60,
    32,
    15,
    44,
    71,
    33,
    42,
    28,
    9,
    49,
    62,
    34,
    50,
    61,
    16,
    64,
    51,
    74,
    45,
    17,
    27,
    35,
    29,
    19,
    77,
    52,
    53,
    65,
    43,
    55,
    94,
    18,
    20,
    54,
    63,
    76,
    56,
    78,
    79,
    80,
    121,
    83,
    81,
    75,
    99,
    122,
    100,
    95,
    111,
    84,
    112,
    101,
    102,
    103,
    123,
    86,
    124,
    82,
    113,
    125,
    96,
    114,
    97,
    115,
    87,
    85,
    89,
    126,
    104,
    105,
    106,
    127,
    88,
    128,
    90,
    98,
    91,
    92,
    129,
    130,
    116,
    107,
    117,
    131,
    132,
    108,
    118,
    133,
    109,
    93,
    134,
    135,
    110,
    119,
    120,
)

VMEM = pl.BlockSpec(memory_space=pltpu.VMEM)
SMEM = pl.BlockSpec(memory_space=pltpu.SMEM)
ANY = pl.BlockSpec(memory_space=pl.ANY)
PARAMS = pltpu.CompilerParams(vmem_limit_bytes=20 * 1024 * 1024)
SMALL = pltpu.CompilerParams(vmem_limit_bytes=20 * 1024 * 1024)


def swap(values, axis, bit):
    pairs = [(i, i ^ (1 << bit)) for i in range(lax.axis_size(axis))]
    return lax.ppermute(values, axis, pairs)


def bit_of(axis, bit):
    return (lax.axis_index(axis) >> bit) & 1


def n_bits(size):
    return size.bit_length() - 1


def pick(flag, first, second):
    return jnp.where(flag == 0, first, second)


def f32_dot(left, right, dims):
    return lax.dot_general(left, right, (dims, ((), ())), preferred_element_type=jnp.float32)


def add_rounded(mine, theirs, parts=1, axis=0):
    shape = list(mine.shape)
    shape[axis] //= parts
    return pl.pallas_call(
        functools.partial(add_kernel, axis),
        out_shape=[bf16(*shape)] * parts,
        in_specs=[VMEM, VMEM],
        out_specs=[VMEM] * parts,
        compiler_params=SMALL,
        name="add",
    )(mine, theirs)


def join(first, second):
    return pl.pallas_call(
        join_kernel,
        out_shape=bf16(2 * first.shape[0], first.shape[1]),
        in_specs=[VMEM, VMEM],
        out_specs=VMEM,
        compiler_params=SMALL,
        name="join",
    )(first, second)


def scalars(*values):
    return jnp.stack([jnp.asarray(value, jnp.int32) for value in values])


def bf16(*shape):
    return jax.ShapeDtypeStruct(shape, jnp.bfloat16)


def store_halves(flag, values, send, keep, axis):
    half = values.shape[axis] // 2
    lower, upper = (values[:half], values[half:]) if axis == 0 else (values[:, :half], values[:, half:])

    @pl.when(flag == 0)
    def _():
        keep[...] = lower
        send[...] = upper

    @pl.when(flag != 0)
    def _():
        keep[...] = upper
        send[...] = lower


def split_kernel(flags, shard, send, keep):
    store_halves(flags[0], shard[...], send, keep, 1)


def delta_kernel(flags, logit, offset, step, send, keep):
    soft_bits = jax.nn.sigmoid(logit[...])
    delta = step[...] * (soft_bits - offset[...].astype(jnp.float32))
    store_halves(flags[0], delta.astype(jnp.bfloat16), send, keep, 1)


def half_kernel(flags, shard, send, keep):
    store_halves(flags[0], shard[...], send, keep, 0)


def pair_kernel(turn, flags, own, theirs, near, far):
    own, theirs = (own[...].T, theirs[...].T) if turn else (own[...], theirs[...])
    half, cols = own.shape[0] // 2, own.shape[1]
    for flag in (0, 1):

        @pl.when(flags[0] == flag)
        def _(flag=flag):
            for lower, out in ((0, near), (half, far)):
                start = half - lower if flag else lower
                for order, (left, right) in enumerate(((own, theirs), (theirs, own))):

                    @pl.when(flags[1] == order)
                    def _(start=start, out=out, left=left, right=right):
                        out[:, :cols] = left[start : start + half]
                        out[:, cols:] = right[start : start + half]


def join_kernel(first, second, out):
    rows = first.shape[0]
    out[:rows, :] = first[...]
    out[rows:, :] = second[...]


def add_kernel(axis, mine, theirs, *outs):
    total = mine[...].astype(jnp.float32) + theirs[...].astype(jnp.float32)
    total = total.astype(jnp.bfloat16)
    size = total.shape[axis] // len(outs)
    for i, out in enumerate(outs):
        at = slice(i * size, (i + 1) * size)
        out[...] = total[at] if axis == 0 else total[:, at]


def rows_kernel(flags, near, back, own, other):
    half, cols = near.shape[0], near.shape[1] // 2
    for z, (first, second) in enumerate(((near, back), (back, near))):

        @pl.when(flags[1] == z)
        def _(first=first, second=second):
            left = jnp.concatenate([first[:, :cols], second[:, :cols]], axis=0).T
            right = jnp.concatenate([first[:, cols:], second[:, cols:]], axis=0).T

            @pl.when(flags[0] == 0)
            def _():
                own[...] = left
                other[...] = right

            @pl.when(flags[0] != 0)
            def _():
                own[...] = right
                other[...] = left


def fetch(flags, pieces, blocks, whole, held, piece_sems, block_sems):
    copies = [
        pltpu.make_async_copy(piece, whole.at[j ^ flags[0]], piece_sems.at[j])
        for j, piece in enumerate(pieces)
    ]
    moved = [
        pltpu.make_async_copy(block, held.at[k], block_sems.at[k])
        for k, block in enumerate(blocks)
    ]
    for copy in copies + moved:
        copy.start()
    return copies, moved


def times_weight(whole, held, waits):
    count, _, wide = whole.shape
    per = count // held.shape[0]
    total = None
    for i in range(count):
        if i % per == 0:
            waits[i // per].wait()
        at = (i % per) * wide
        part = f32_dot(whole[i], held[i // per, :, at : at + wide], ((1,), (1,)))
        total = part if total is None else total + part
    return total


def fisher_kernel(count, *refs):
    flags, pieces, refs = refs[0], refs[1 : count + 1], refs[count + 1 :]
    blocks, (gate, fisher, total, *scratch) = refs[:-7], refs[-7:]
    whole, held = scratch[:2]
    copies, moved = fetch(flags, pieces, blocks, *scratch)
    for copy in copies:
        copy.wait()
    grads = times_weight(whole, held, moved)
    value = ((grads * gate[...].astype(jnp.float32)) ** 2).astype(jnp.bfloat16)
    fisher[...] = value
    total[0, 0] = jnp.sum(value.astype(jnp.float32))


def residual_kernel(count, *refs):
    flags, pieces, refs = refs[0], refs[1 : count + 1], refs[count + 1 :]
    blocks, (fisher, weighted, total, *scratch) = refs[:-7], refs[-7:]
    whole, held = scratch[:2]
    copies, moved = fetch(flags, pieces, blocks, *scratch)
    for copy in copies:
        copy.wait()
    residual = times_weight(whole, held, moved)
    value = fisher[...].astype(jnp.float32) * residual
    weighted[...] = value.astype(jnp.bfloat16)
    total[0, 0] = jnp.sum(value * residual)


def grad_kernel(count, wanted, flags, *refs):
    refs, (held, sems) = refs[:-2], refs[-2:]
    grads, refs = refs[-len(wanted) :], refs[: -len(wanted)]
    half = len(refs) // 2 - 1
    blocks, weighted = refs[: 2 * half], refs[2 * half :]
    wide = grads[0].shape[1]
    per = count // half

    def copies(number, i):
        return [
            pltpu.make_async_copy(
                blocks[chunk * half + i // per], held.at[2 * number + chunk], sems.at[2 * number + chunk]
            )
            for chunk in (0, 1)
        ]

    for number, j in enumerate(wanted):
        for i in range(count):

            @pl.when(flags[0] == i ^ j)
            def _(number=number, i=i):
                for copy in copies(number, i):
                    copy.start()

    for number, j in enumerate(wanted):
        for i in range(count):

            @pl.when(flags[0] == i ^ j)
            def _(number=number, i=i):
                at = (i % per) * wide
                first, second = copies(number, i)
                first.wait()
                part = f32_dot(weighted[0][...], held[2 * number, :, at : at + wide], ((1,), (0,)))
                second.wait()
                part += f32_dot(
                    weighted[1][...], held[2 * number + 1, :, at : at + wide], ((1,), (0,))
                )
                grads[number][...] = part.astype(jnp.bfloat16)


def stack_kernel(flags, near, back, own, other):
    half, cols = near.shape[0], near.shape[1] // 2
    for z, (first, second) in enumerate(((near, back), (back, near))):

        @pl.when(flags[1] == z)
        def _(first=first, second=second):
            for at, out in enumerate((own, other)):
                out[:half, :] = first[:, at * cols : (at + 1) * cols]
                out[half:, :] = second[:, at * cols : (at + 1) * cols]


def output_kernel(count, *refs):
    flags, ups, downs = refs[0], refs[1 : count + 1], refs[count + 1 : 2 * count + 1]
    refs = refs[2 * count + 1 :]
    blocks, (gate, keep, send, *scratch) = refs[:-8], refs[-8:]
    whole, held, back, sems, block_sems = scratch
    copies, moved = fetch(flags, ups, blocks, whole, held, sems.at[0], block_sems)
    later, _ = fetch(flags, downs, (), back, held, sems.at[1], block_sems)
    for copy in copies:
        copy.wait()
    hidden = times_weight(whole, held, moved) * gate[...].astype(jnp.float32)
    hidden = hidden.astype(jnp.bfloat16)
    for copy in later:
        copy.wait()
    feats, wide = held.shape[2], whole.shape[2]
    per = count // held.shape[0]
    for i in range(count):
        k = i // per
        at = (k >> 1) * feats + (i % per) * wide
        out = send if k & 1 else keep
        part = f32_dot(hidden, back[i], ((0,), (0,)))
        out[:, at : at + wide] = part.astype(jnp.bfloat16)


class Plan:
    def __init__(self):
        self.steps, self.got, self.flying, self.token = {}, {}, {}, None

    def tie(self, values):
        values, self.token = lax.optimization_barrier((values, self.token))
        return values

    def exchange(self, name, axis, bit, source):
        def start():
            self.flying[name] = swap(self.tie(source()), axis, bit)

        def wait():
            self.got[name] = self.tie(self.flying.pop(name))

        self.steps["s " + name], self.steps["w " + name] = start, wait

    def compute(self, name, function, tied=True):
        def run():
            values = function()
            self.got[name] = self.tie(values) if tied else values

        self.steps["c " + name] = run

    def run(self, token, order):
        self.token = token
        steps = list(self.steps.values())
        if len(order) != len(steps):
            order = range(len(steps))
        for number in order:
            steps[number]()
        return self.got


def plan_pair(plan, name, first, order, turn):
    got = plan.got
    plan.compute("p" + name, first)
    plan.exchange(name + "_y", "dp", 0, lambda: got["p" + name][0])

    def pair():
        own, theirs = got["p" + name][1], got[name + "_y"]
        rows, cols = own.shape[::-1] if turn else own.shape
        out = bf16(rows // 2, 2 * cols)
        return pl.pallas_call(
            functools.partial(pair_kernel, turn),
            out_shape=(out, out),
            in_specs=[SMEM, VMEM, VMEM],
            out_specs=(VMEM, VMEM),
            compiler_params=SMALL,
            name="pair",
        )(scalars(bit_of("dp", 1), order), own, theirs)

    plan.compute("k" + name, pair)
    plan.exchange(name + "_zl", "dp", 1, lambda: got["k" + name][1])


def plan_weight(plan, name, first, nb):
    got = plan.got
    plan_pair(plan, name, first, bit_of("dp", 0), True)
    pieces = [lambda: got["k" + name][0], lambda: got[name + "_zl"]]
    for bit in range(2, nb):
        for piece in list(pieces):
            key = name + "_h" + str(len(pieces) - 2)
            plan.exchange(key, "dp", bit, piece)
            pieces.append(lambda key=key: got[key])
    return lambda: [piece() for piece in pieces]


def plan_tokens(plan, name, shard, nt):
    got, chunks = plan.got, {}
    plan.exchange(name + "b_zl", "dp", 1, lambda: shard)
    for chunk, own in (("a", lambda: shard), ("b", lambda: got[name + "b_zl"])):
        key = name + chunk
        plan.exchange(key + "_y", "dp", 0, own)
        plan.compute(
            "c" + key,
            lambda own=own, key=key: join(own(), got[key + "_y"]),
        )
        blocks = ["c" + key]
        for bit in range(nt - 1, -1, -1):
            new = []
            for index, block in enumerate(blocks):
                part = key + "_t" + str(bit) + str(index)
                plan.exchange(part, "tensor", bit, lambda block=block: got[block])
                new += [block, part]
            blocks = new
        chunks[chunk] = blocks
    return lambda chunk: [got[key] for key in chunks[chunk]]


def plan_collect(plan, name, near, away):
    got = plan.got
    y, z = bit_of("dp", 0), bit_of("dp", 1)
    plan.exchange(name + "_zl", "dp", 1, away)

    def stack():
        out = bf16(2 * near().shape[0], near().shape[1] // 2)
        return pl.pallas_call(
            stack_kernel,
            out_shape=(out, out),
            in_specs=[SMEM, VMEM, VMEM],
            out_specs=(VMEM, VMEM),
            compiler_params=SMALL,
            name="stack",
        )(scalars(y, z), near(), got[name + "_zl"])

    plan.compute("p" + name, stack)
    plan.exchange(name + "_y", "dp", 0, lambda: got["p" + name][1])

    def whole():
        own, theirs = got["p" + name][0], got[name + "_y"]
        return jnp.concatenate([pick(y, own, theirs), pick(y, theirs, own)], axis=0)

    return whole


def plan_scatter(plan, full, nb):
    got = plan.got
    y, z = bit_of("dp", 0), bit_of("dp", 1)
    half, number, pieces = 1 << (nb - 2), 0, []
    for index in range(2 * half):
        pieces.append(lambda index=index: full(index))
    for bit in range(nb - 1, 1, -1):
        half = len(pieces) // 2
        sums = []
        for index in reversed(range(half)):
            name = "R_h" + str(number)
            plan.exchange(name, "dp", bit, pieces[half + index])
            plan.compute(
                "a" + str(number),
                lambda mine=pieces[index], name=name: add_rounded(mine(), got[name])[0],
            )
            sums.insert(0, lambda key="a" + str(number): got[key])
            number += 1
        pieces = sums
    near, away = pieces
    plan.exchange("R_zl", "dp", 1, away)

    def rows():
        out = bf16(near().shape[1] // 2, 2 * near().shape[0])
        return pl.pallas_call(
            rows_kernel,
            out_shape=(out, out),
            in_specs=[SMEM, VMEM, VMEM],
            out_specs=(VMEM, VMEM),
            compiler_params=SMALL,
            name="rows",
        )(scalars(y, z), near(), got["R_zl"])

    plan.compute("ry", rows)
    plan.exchange("R_y", "dp", 0, lambda: got["ry"][1])

    def whole():
        own, theirs = got["ry"][0], got["R_y"]
        return jnp.concatenate([pick(y, own, theirs), pick(y, theirs, own)], axis=1)

    return whole


def plan_output(plan, part, tok, nt):
    got = plan.got
    for chunk in "ba":
        key = "O" + chunk
        plan.compute("kC" + chunk, lambda chunk=chunk: part(chunk))
        plan.exchange(key + "_t0", "tensor", 0, lambda chunk=chunk: got["kC" + chunk][1])
        last = "o0" + chunk
        plan.compute(
            last,
            lambda chunk=chunk, key=key: add_rounded(
                got["kC" + chunk][0], got[key + "_t0"], 2, int(nt > 1)
            ),
        )
        for bit in range(nt - 1, 0, -1):
            name, step = key + "_t" + str(bit), "o" + str(bit) + chunk
            plan.exchange(name, "tensor", bit, lambda last=last: got[last][1])
            plan.compute(
                step,
                lambda last=last, name=name, bit=bit: add_rounded(
                    got[last][0], got[name], 2, int(bit > 1)
                ),
            )
            last = step
        plan.exchange(key + "_y", "dp", 0, lambda last=last: got[last][1])
        plan.compute(
            "oy" + chunk,
            lambda last=last, key=key: add_rounded(got[last][0], got[key + "_y"])[0],
        )
        if chunk == "b":
            plan.exchange("O_zl", "dp", 1, lambda: got["oyb"])
    return lambda: add_rounded(got["oya"], got["O_zl"])[0]


def body(
    block_input, gate_act, grad_out, up_weight, down_weight, quant_step, round_logit, grid_offset
):
    n_dp, n_tensor = lax.axis_size("dp"), lax.axis_size("tensor")
    nb, nt = n_bits(n_dp), n_bits(n_tensor)
    tok, cols = gate_act.shape
    half, quarter = cols // 2, cols // 4
    rows = up_weight.shape[0]
    feats = block_input.shape[1]
    depth = rows * n_dp
    count = n_dp // 2
    y = bit_of("dp", 0)
    shift = (lax.axis_index("dp") >> 1) ^ (lax.axis_index("tensor") << (nb - 1 - nt))

    soft_bits = jax.nn.sigmoid(round_logit)
    centered = 2.0 * soft_bits - 1.0
    reg_local = jnp.sum(1.0 - (centered * centered) ** 2)

    def split(name, kernel, out, *operands):
        return pl.pallas_call(
            kernel,
            out_shape=(out, out),
            in_specs=[SMEM] + [VMEM] * len(operands),
            out_specs=(VMEM, VMEM),
            compiler_params=SMALL,
            name=name,
        )(scalars(y), *operands)

    plan = Plan()
    got = plan.got
    out = bf16(rows, half)
    down = plan_weight(plan, "D", lambda: split("split", split_kernel, out, down_weight.T), nb)
    grads = plan_tokens(plan, "G", grad_out, nt)
    plan_pair(
        plan, "g", lambda: split("split", half_kernel, bf16(half, tok), gate_act.T), 0, False
    )
    gate = lambda chunk: got["kg"][0] if chunk == "a" else got["g_zl"]
    delta = plan_weight(
        plan,
        "T",
        lambda: split(
            "delta", delta_kernel, out, round_logit, grid_offset, quant_step[None, :]
        ),
        nb,
    )
    features = plan_tokens(plan, "X", block_input, nt)
    up = plan_weight(plan, "U", lambda: split("split", split_kernel, out, up_weight), nb)
    whole = pltpu.VMEM((count, quarter, 2 * rows), jnp.bfloat16)
    held = pltpu.VMEM((n_tensor, 2 * tok, feats), jnp.bfloat16)
    sems = pltpu.SemaphoreType.DMA

    def matmuls(name, kernel, out_shape, out_specs, scratch, *operands):
        return pl.pallas_call(
            functools.partial(kernel, count),
            out_shape=out_shape,
            in_specs=[SMEM] + [ANY] * (len(operands) - 1) + [VMEM],
            out_specs=out_specs,
            scratch_shapes=scratch,
            compiler_params=PARAMS,
            name=name,
        )(scalars(shift), *operands)

    simple = [whole, held, sems((count,)), sems((n_tensor,))]
    one = jax.ShapeDtypeStruct((1, 1), jnp.float32)
    for chunk in "ab":
        plan.compute(
            "kA" + chunk,
            lambda chunk=chunk: matmuls(
                "fisher_matmul",
                fisher_kernel,
                (bf16(quarter, 2 * tok), one),
                (VMEM, SMEM),
                simple,
                *down(),
                *grads(chunk),
                gate(chunk),
            ),
        )
    fisher = lambda chunk: got["kA" + chunk][0]
    for chunk in "ab":
        plan.compute(
            "kR" + chunk,
            lambda chunk=chunk: matmuls(
                "residual_matmul",
                residual_kernel,
                (bf16(quarter, 2 * tok), one),
                (VMEM, SMEM),
                simple,
                *delta(),
                *features(chunk),
                fisher(chunk),
            ),
        )

    def make_grad(wanted):
        operands = *features("a"), *features("b"), got["kRa"][0], got["kRb"][0]
        return pl.pallas_call(
            functools.partial(grad_kernel, count, wanted),
            out_shape=[bf16(quarter, 2 * rows)] * len(wanted),
            in_specs=[SMEM] + [ANY] * (len(operands) - 2) + [VMEM, VMEM],
            out_specs=[VMEM] * len(wanted),
            scratch_shapes=[
                pltpu.VMEM((2 * len(wanted), 2 * tok, feats), jnp.bfloat16),
                sems((2 * len(wanted),)),
            ],
            compiler_params=PARAMS,
            name="grad_matmul",
        )(scalars(shift), *operands)

    parts = [(j,) for j in reversed(range(count // 2, count))] + [tuple(range(count // 2))]
    where = {}
    for number, wanted in enumerate(parts):
        plan.compute("r" + str(number), lambda wanted=wanted: make_grad(wanted))
        for at, j in enumerate(wanted):
            where[j] = "r" + str(number), at
    grad_rows = plan_scatter(plan, lambda j: got[where[j][0]][where[j][1]], nb)
    fisher_rows = plan_collect(plan, "f", lambda: fisher("a"), lambda: fisher("b"))
    pair = bf16(2 * tok, depth // 2)
    out_rows = plan_output(
        plan,
        lambda chunk: matmuls(
            "output_matmul",
            output_kernel,
            (pair, pair),
            (VMEM, VMEM),
            [whole, held, whole, sems((2, count)), sems((n_tensor,))],
            *up(),
            *down(),
            *features(chunk),
            gate(chunk),
        ),
        tok,
        nt,
    )

    last = lambda: jnp.concatenate(
        [got["kAa"][1] + got["kAb"][1], got["kRa"][1] + got["kRb"][1], reg_local[None, None]], axis=1
    )
    for axis, bits in (("dp", nb), ("tensor", nt)):
        for bit in range(bits):
            name = "s_" + axis + str(bit)
            plan.exchange(name, axis, bit, last)
            plan.compute("q" + name, lambda last=last, name=name: last() + got[name], tied=False)
            last = lambda name=name: got["q" + name]

    plan.run(lax.axis_index("dp"), ORDER)

    sums = last()[0]
    fisher_sum, recon_total, reg_total = sums[0], sums[1], sums[2]
    total_cells = n_dp * n_tensor * tok * cols
    weight_cells = depth * n_tensor * cols
    fisher_mean = fisher_sum / total_cells
    sig_slope = soft_bits * (1.0 - soft_bits)
    grad_logit = (
        grad_rows().astype(jnp.float32)
        * (2.0 / fisher_mean)
        * quant_step[None, :]
        * sig_slope
        - reg_weight * 8.0 * centered**3 * sig_slope
    )
    loss = recon_total / (fisher_mean * total_cells) + reg_weight * reg_total / weight_cells
    loss = jnp.where(plan.token < 0, -loss, loss)
    return (out_rows(), fisher_rows().T, grad_logit, loss)


def solution(mesh):
    placed = (
        P("dp", "tensor"),
        P("dp", "tensor"),
        P("dp", "tensor"),
        P("dp", "tensor"),
        P("tensor", "dp"),
        P("tensor"),
        P("dp", "tensor"),
        P("dp", "tensor"),
    )
    return jax.shard_map(
        body,
        mesh=mesh,
        in_specs=placed,
        out_specs=(P("dp", "tensor"), P("dp", "tensor"), P("dp", "tensor"), P()),
        check_vma=False,
    )
```
